128 devices in a mesh: grp: 8 (over z, core), sub: 16 (over y, x).
Axes of the slice: x: 4, y: 4, z: 4, core: 2. Of those that a mesh axis runs over, the one named last changes fastest.
Arguments:
- features: bfloat16 [512, 8, 8, 512], P(('grp', 'sub')), may hold values from -6 to 6
- conv_weight: bfloat16 [27, 64, 64], replicated, may hold values from -0.15625 to 0.15625
- down_weight: bfloat16 [64, 128], replicated, may hold values from -0.75 to 0.75
- cotangent: bfloat16 [128, 512, 128], P(('grp', 'sub')), may hold values from -24 to 24
- src_table: int32 [512, 26], P(('grp', 'sub')), may hold values from -1 to 535, as said below
- send_list: int32 [128, 128, 4], P(('grp', 'sub')), may hold values from -1 to 23, as said below
- child_map: int32 [512], P(('grp', 'sub')), may hold values from -1 to 1023, as said below
Outputs:
- coarse: bfloat16 [128, 512, 128], P(('grp', 'sub'))
- grad_input: bfloat16 [512, 8, 8, 512], P(('grp', 'sub'))
- grad_conv: float32 [27, 64, 64], replicated
- grad_down: float32 [64, 128], replicated
The draws below stay inside these ranges and needn't reach their ends.
Inputs may be any that keep to these rules, and one draw needn't show every extreme that they name: `src_table`: A brick slot is live where child_map >= 0; every device has 2 to 4 live slots, the lowest ones, and some device has 4. -1 or a code as in the reference program; local codes name live slots; remote codes name used send slots. `send_list`: entry [p, r, k] is -1 or 6 times a live slot of device p plus a face number; the used slots of [p, r] come first; device p sends faces only to devices within 16 of p in cyclic device order or exactly 64 away, at most 4 to one device, and some pair sends exactly 4 in every draw. `child_map`: -1 exactly on slots that are not live; live bricks of one super-range have distinct values.
All inputs are finite; a program needn't handle non-finite values.
Results may differ from the reference program's by a relative error of at most 0.0058.
Values may be sent and summed in bfloat16 or wider, within the bound.
A program may use at most 128 MiB of HBM per device.

```python
import jax
import jax.numpy as jnp
import numpy as np
from jax import lax

C = 64
CC = 128
BCAP = 4
KSEND = 4
CB = 1
BRICKS = 512
CBRICKS = 128
N_GRP = 8
N_SUB = 16


def face_codes():
    table = []
    for step_x in (-1, 0, 1):
        for step_y in (-1, 0, 1):
            for step_z in (-1, 0, 1):
                offset = (step_x, step_y, step_z)
                if step_x != 0 or step_y != 0 or step_z != 0:
                    first_axis = 0 if step_x != 0 else 1 if step_y != 0 else 2
                    table.append(2 * first_axis + (0 if offset[first_axis] > 0 else 1))
    return np.array(table, np.int32)


def layout(key):
    peer_count = N_GRP * N_SUB
    subkeys = jax.random.split(key, 10)
    lowest = BCAP // 2
    counts = lowest + jax.random.randint(subkeys[0], (peer_count,), 0, BCAP - lowest + 1)
    fullest = jax.random.randint(subkeys[1], (), 0, peer_count)
    counts = jnp.where(jnp.arange(peer_count) == fullest, BCAP, counts)
    raw_pairs = jax.random.randint(subkeys[2], (peer_count, peer_count - 1), 0, KSEND + 1)
    step_num = jnp.arange(1, peer_count)
    distance = jnp.minimum(step_num, peer_count - step_num)
    reachable = jnp.logical_or(distance <= N_SUB, step_num == peer_count // 2)
    raw_pairs = jnp.where(reachable[None, :], raw_pairs, 0)
    far_row = jax.random.randint(subkeys[9], (), 0, peer_count)
    raw_pairs = raw_pairs.at[far_row].set(0)
    raw_pairs = raw_pairs.at[far_row, peer_count // 2 - 1].set(KSEND)
    forced = jax.random.randint(subkeys[3], (), 0, peer_count)
    raw_pairs = raw_pairs.at[forced, 0].set(KSEND)
    raw_pairs = raw_pairs.at[peer_count - 2, 0].set(KSEND)
    below_full = (fullest + peer_count - 1) % peer_count
    raw_pairs = raw_pairs.at[below_full, 0].set(KSEND)
    capacity = 13 * counts
    pair_count = jnp.where(jnp.cumsum(raw_pairs, axis=1) <= capacity[:, None], raw_pairs, 0)
    upper_cum = jnp.cumsum(pair_count, axis=1)
    lower_cum = upper_cum - pair_count
    remote_total = upper_cum[:, -1]
    positions = BCAP * 26
    position = jnp.arange(positions)
    is_live = position[None, :] // 26 < counts[:, None]
    scores = jnp.where(is_live, 0, 1 << 28) + jax.random.randint(subkeys[4], (peer_count, positions), 0, 1 << 14) * 4096 + position[None, :]
    perm_order = jnp.argsort(scores, axis=1).astype(jnp.int32)
    perm_rank = jnp.argsort(perm_order, axis=1).astype(jnp.int32)
    faces_table = jnp.asarray(face_codes())
    face_of = faces_table[position % 26]
    offset_num = jnp.sum(upper_cum[:, None, :] <= perm_rank[:, :, None], axis=2)
    offset_num = jnp.minimum(offset_num, peer_count - 2)
    within = perm_rank - jnp.take_along_axis(lower_cum, offset_num, axis=1)
    source = (jnp.arange(peer_count)[:, None] + offset_num + 1) % peer_count
    remote_code = BCAP * 6 + source * KSEND + within
    local_slot = jax.random.randint(subkeys[5], (peer_count, positions), 0, 1 << 16) % counts[:, None]
    local_code = local_slot * 6 + face_of[None, :]
    keep_local = jax.random.randint(subkeys[6], (peer_count, positions), 0, 4) > 0
    is_remote = perm_rank < remote_total[:, None]
    is_local = jnp.logical_and(jnp.logical_and(jnp.logical_not(is_remote), is_live), keep_local)
    source_table = jnp.where(is_remote, remote_code, jnp.where(is_local, local_code, -1)).reshape(peer_count * BCAP, 26)
    slot_num = jnp.arange(KSEND)
    starts = lower_cum[:, :, None] + slot_num[None, None, :]
    is_used = slot_num[None, None, :] < pair_count[:, :, None]
    picked = jnp.take_along_axis(perm_order, jnp.minimum(starts, positions - 1).reshape(peer_count, -1), axis=1).reshape(starts.shape)
    sender = (jnp.arange(peer_count)[:, None, None] + jnp.arange(1, peer_count)[None, :, None]) % peer_count
    sender = jnp.broadcast_to(sender, starts.shape)
    sender_slot = jax.random.randint(subkeys[7], starts.shape, 0, 1 << 16) % counts[sender]
    send_value = sender_slot * 6 + faces_table[picked % 26]
    receiver = jnp.broadcast_to(jnp.arange(peer_count)[:, None, None], starts.shape)
    slot_full = jnp.broadcast_to(slot_num[None, None, :], starts.shape)
    send_table = jnp.full((peer_count, peer_count, KSEND), -1, jnp.int32).at[jnp.where(is_used, sender, peer_count), receiver, slot_full].set(send_value.astype(jnp.int32), mode='drop')
    send_table = send_table.at[fullest, below_full, 0].set(6 * BCAP - 1)
    group_counts = counts.reshape(N_GRP, N_SUB)
    before = jnp.cumsum(group_counts, axis=1) - group_counts
    child_index = before[:, :, None] + jnp.arange(BCAP)[None, None, :]
    spot_count = N_SUB * CB * 64
    spot_score = jax.random.randint(subkeys[8], (N_GRP, spot_count), 0, 1 << 14) * 4096 + jnp.arange(spot_count)[None, :]
    spot_order = jnp.argsort(spot_score, axis=1).astype(jnp.int32)
    chosen = jnp.take_along_axis(spot_order, jnp.minimum(child_index, spot_count - 1).reshape(N_GRP, -1), axis=1).reshape(child_index.shape)
    child_codes = jnp.where(jnp.arange(BCAP)[None, None, :] < group_counts[:, :, None], chosen, -1).reshape(-1)
    return (source_table.astype(jnp.int32), send_table, child_codes.astype(jnp.int32))


def draw_src_table(key, part):
    return layout(key)[0]


def draw_send_list(key, part):
    return layout(key)[1]


def draw_child_map(key, part):
    return layout(key)[2]


def block_scale(stream_key, shape, cuts, least, largest):
    gain, own = 1.0, jax.random.fold_in(stream_key, 6)
    for dim, blocks in cuts:
        draws = jnp.exp(jax.random.uniform(jax.random.fold_in(own, dim), (blocks,), jnp.float32, least / len(cuts), largest / len(cuts)))
        gain = gain * jnp.repeat(draws, shape[dim] // blocks).reshape([-1 if axis == dim else 1 for axis in range(len(shape))])
    return gain


def scatter_about(rng, shape, spread, reach, cuts=(), held_as=jnp.bfloat16):
    values = jax.random.normal(rng, shape, jnp.float32) * spread
    if len(cuts) > 0:
        values = block_scale(rng, shape, cuts, -0.22, 0.18) * values
    return jnp.clip(values, min=-reach, max=reach).astype(held_as)


def setup_inputs(seed: int = 0) -> dict:
    arg_keys = jax.random.split(jax.random.key(seed), 8)
    return {
        "features": scatter_about(arg_keys[0], (BRICKS, 8, 8, 8 * C), 1.0, 6.0, ((0, 128),)),
        "conv_weight": scatter_about(arg_keys[1], (27, C, C), (27 * C) ** -0.5, 0.15625),
        "down_weight": scatter_about(arg_keys[2], (C, CC), C ** -0.5, 0.75),
        "cotangent": scatter_about(arg_keys[3], (CBRICKS, 512, CC), 4.0, 24.0, ((0, 128),)),
        "src_table": draw_src_table(jax.random.fold_in(arg_keys[7], 71), 0),
        "send_list": draw_send_list(jax.random.fold_in(arg_keys[7], 71), 0),
        "child_map": draw_child_map(jax.random.fold_in(arg_keys[7], 71), 0),
    }


def offsets():
    result = []
    for step_x in (-1, 0, 1):
        for step_y in (-1, 0, 1):
            for step_z in (-1, 0, 1):
                if step_x != 0 or step_y != 0 or step_z != 0:
                    result.append((step_x, step_y, step_z))
    return result

def face_axis_of(offset):
    return 0 if offset[0] != 0 else 1 if offset[1] != 0 else 2

def pad_range(step_value):
    if step_value > 0:
        return (9, 10)
    if step_value < 0:
        return (0, 1)
    return (1, 9)

def slab_range(step_value):
    if step_value > 0:
        return (0, 1)
    if step_value < 0:
        return (7, 8)
    return (0, 8)

def brick_faces(bricks):
    return jnp.stack([bricks[:, 0], bricks[:, 7], bricks[:, :, 0], bricks[:, :, 7], bricks[:, :, :, 0], bricks[:, :, :, 7]], axis=1)

def place_slabs(bricks, slabs):
    padded = jnp.pad(bricks, ((0, 0), (1, 1), (1, 1), (1, 1), (0, 0)))
    for number, offset in enumerate(offsets()):
        axis_face = face_axis_of(offset)
        others = [axis_num for axis_num in range(3) if axis_num != axis_face]
        first_span = slab_range(offset[others[0]])
        second_span = slab_range(offset[others[1]])
        slab_part = slabs[:, number, first_span[0]:first_span[1], second_span[0]:second_span[1], :]
        slab_part = jnp.expand_dims(slab_part, axis_face + 1)
        corner = (0, pad_range(offset[0])[0], pad_range(offset[1])[0], pad_range(offset[2])[0], 0)
        padded = lax.dynamic_update_slice(padded, slab_part, corner)
    return padded

def rim_grads(dpadded):
    result = []
    for offset in offsets():
        axis_face = face_axis_of(offset)
        edge_spans = [pad_range(step_value) for step_value in offset]
        region = dpadded[:, edge_spans[0][0]:edge_spans[0][1], edge_spans[1][0]:edge_spans[1][1], edge_spans[2][0]:edge_spans[2][1], :]
        region = jnp.squeeze(region, axis_face + 1)
        others = [axis_num for axis_num in range(3) if axis_num != axis_face]
        first_span = slab_range(offset[others[0]])
        second_span = slab_range(offset[others[1]])
        blank = jnp.zeros((region.shape[0], 8, 8, region.shape[-1]), dpadded.dtype)
        result.append(lax.dynamic_update_slice(blank, region, (0, first_span[0], second_span[0], 0)))
    return jnp.stack(result, axis=1)

def shift_window(padded, shift_x, shift_y, span_size):
    layers = [padded[:, shift_x:shift_x + span_size, shift_y:shift_y + span_size, shift_z:shift_z + span_size, :] for shift_z in range(3)]
    joined = jnp.concatenate(layers, axis=-1)
    return joined.reshape(-1, joined.shape[-1])

def conv_sum(padded, weight_flat, span_size):
    channels = padded.shape[-1]
    running = None
    for shift_x in range(3):
        for shift_y in range(3):
            row_start = (9 * shift_x + 3 * shift_y) * channels
            product = jnp.dot(shift_window(padded, shift_x, shift_y, span_size), weight_flat[row_start:row_start + 3 * channels], preferred_element_type=jnp.float32)
            running = product if running is None else running + product
    return running

def weight_grad(padded, grad_rows):
    pieces = []
    for shift_x in range(3):
        for shift_y in range(3):
            pieces.append(lax.dot_general(shift_window(padded, shift_x, shift_y, 8), grad_rows, (((0,), (0,)), ((), ())), preferred_element_type=jnp.float32))
    return jnp.concatenate(pieces, axis=0)

def pool_tiles(preact, count):
    channels = preact.shape[-1]
    activated = jax.nn.silu(preact).reshape(count, 2, 4, 2, 4, 2, 4, channels)
    return lax.optimization_barrier(jnp.mean(activated, axis=(2, 4, 6))).astype(jnp.bfloat16).reshape(count, 8 * channels)

def spread_tiles(tile_grad, count):
    channels = tile_grad.shape[-1] // 8
    shaped = tile_grad.reshape(count, 2, 1, 2, 1, 2, 1, channels)
    return (jnp.broadcast_to(shaped, (count, 2, 4, 2, 4, 2, 4, channels)) / 64.0).reshape(count * 512, channels)

def silu_slope(values):
    sigma = jax.nn.sigmoid(values)
    return sigma * (1.0 + values * (1.0 - sigma))

def to_voxels(tiles_rows, count):
    channels = tiles_rows.shape[-1] // 8
    shaped = tiles_rows.reshape(count, 4, 4, 4, 2, 2, 2, channels).transpose(0, 1, 4, 2, 5, 3, 6, 7)
    return shaped.reshape(count, 512, channels)

def to_tiles(voxels, count):
    channels = voxels.shape[-1]
    shaped = voxels.reshape(count, 4, 2, 4, 2, 4, 2, channels).transpose(0, 1, 3, 5, 2, 4, 6, 7)
    return shaped.reshape(count * 64, 8 * channels)

def add_faces(interior, face_grad):
    interior = interior.at[:, 0].add(face_grad[:, 0])
    interior = interior.at[:, 7].add(face_grad[:, 1])
    interior = interior.at[:, :, 0].add(face_grad[:, 2])
    interior = interior.at[:, :, 7].add(face_grad[:, 3])
    interior = interior.at[:, :, :, 0].add(face_grad[:, 4])
    interior = interior.at[:, :, :, 7].add(face_grad[:, 5])
    return interior

def reference(features, conv_weight, down_weight, cotangent, src_table, send_list, child_map):
    peer_count = N_GRP * N_SUB
    channels = C
    bricks = features.reshape(BRICKS, 8, 8, 8, channels)
    face_rows = brick_faces(bricks).reshape(BRICKS * 6, 8, 8 * channels)
    owner_dev = jnp.arange(BRICKS, dtype=jnp.int32) // BCAP
    has_source = src_table >= 0
    is_local = src_table < BCAP * 6
    remote = jnp.maximum(src_table - BCAP * 6, 0)
    peer_num = jnp.minimum(remote // KSEND, peer_count - 1)
    slot_num = remote % KSEND
    sent_code = send_list[peer_num, owner_dev[:, None], slot_num]
    gather_rows = jnp.where(is_local, owner_dev[:, None] * (BCAP * 6) + src_table, peer_num * (BCAP * 6) + sent_code)
    gather_rows = jnp.where(has_source, gather_rows, 0).astype(jnp.int32)
    weight_flat = conv_weight.reshape(27 * channels, channels)
    flipped = jnp.flip(conv_weight, 0).transpose(0, 2, 1).reshape(27 * channels, channels)
    zero_face = jnp.zeros((), face_rows.dtype)

    def build_padded(own_bricks, row_codes, present):
        slabs = jnp.where(present[:, :, None, None], face_rows[row_codes], zero_face).reshape(BCAP, 26, 8, 8, channels)
        return place_slabs(own_bricks, slabs)
    by_device = (bricks.reshape(peer_count, BCAP, 8, 8, 8, channels), gather_rows.reshape(peer_count, BCAP, 26), has_source.reshape(peer_count, BCAP, 26))
    preact = lax.map(lambda inputs: conv_sum(build_padded(inputs[0], inputs[1], inputs[2]), weight_flat, 8), by_device)
    preact = preact.reshape(BRICKS * 512, channels)
    pooled = pool_tiles(preact, BRICKS)
    group_num = owner_dev // N_SUB
    spots_total = CBRICKS * 64
    coarse_pos = jnp.where(child_map >= 0, group_num * (N_SUB * CB * 64) + child_map, spots_total).astype(jnp.int32)
    coarse_tiles = jnp.zeros((spots_total, 8 * channels), jnp.bfloat16).at[coarse_pos].add(pooled, mode='drop')
    coarse_in = to_voxels(coarse_tiles, CBRICKS).reshape(CBRICKS * 512, channels)
    coarse = jnp.dot(coarse_in, down_weight, preferred_element_type=jnp.float32).astype(jnp.bfloat16)
    grad_rows = cotangent.reshape(CBRICKS * 512, CC)
    grad_down = lax.dot_general(coarse_in, grad_rows, (((0,), (0,)), ((), ())), preferred_element_type=jnp.float32)
    coarse_grad = jnp.dot(grad_rows, down_weight.T, preferred_element_type=jnp.float32).astype(jnp.bfloat16)
    grad_tiles = to_tiles(coarse_grad.reshape(CBRICKS, 512, channels), CBRICKS)
    tile_grad = jnp.where((child_map >= 0)[:, None], grad_tiles[jnp.minimum(coarse_pos, spots_total - 1)], jnp.zeros((), grad_tiles.dtype)).astype(jnp.float32)
    pre_grad = (spread_tiles(tile_grad, BRICKS) * silu_slope(preact)).astype(jnp.bfloat16)
    peer_ids = jnp.arange(peer_count, dtype=jnp.int32)

    def backward_step(carry, inputs):
        face_acc, conv_acc = carry
        padded = build_padded(inputs[0], inputs[1], inputs[2])
        grad_part = inputs[3]
        codes = inputs[4]
        device_num = inputs[5]
        conv_part = weight_grad(padded, grad_part)
        grad_padded = jnp.pad(grad_part.reshape(BCAP, 8, 8, 8, channels), ((0, 0), (2, 2), (2, 2), (2, 2), (0, 0)))
        dpadded = conv_sum(grad_padded, flipped, 10).reshape(BCAP, 10, 10, 10, channels)
        slab_terms = rim_grads(dpadded).reshape(BCAP, 26, 8, 8 * channels)
        present = codes >= 0
        local_mask = jnp.logical_and(present, codes < BCAP * 6)
        remote_mask = jnp.logical_and(present, codes >= BCAP * 6)
        local_target = jnp.where(local_mask, device_num * (BCAP * 6) + codes, BRICKS * 6).astype(jnp.int32)
        face_acc = face_acc.at[local_target].add(slab_terms, mode='drop')
        remote_target = jnp.where(remote_mask, codes - BCAP * 6, peer_count * KSEND).astype(jnp.int32)
        remote_sum = jnp.zeros((peer_count * KSEND, 8, 8 * channels), jnp.float32).at[remote_target].add(slab_terms, mode='drop')
        rounded = lax.optimization_barrier(remote_sum.astype(jnp.bfloat16)).astype(jnp.float32)
        codes_back = lax.dynamic_index_in_dim(send_list, device_num, 1, keepdims=False)
        owner_target = jnp.where(codes_back >= 0, peer_ids[:, None] * (BCAP * 6) + codes_back, BRICKS * 6).astype(jnp.int32).reshape(-1)
        face_acc = face_acc.at[owner_target].add(rounded, mode='drop')
        return ((face_acc, conv_acc + conv_part), dpadded[:, 1:9, 1:9, 1:9])
    start = (jnp.zeros((BRICKS * 6, 8, 8 * channels), jnp.float32), jnp.zeros((27 * channels, channels), jnp.float32))
    xs = by_device + (pre_grad.reshape(peer_count, BCAP * 512, channels), src_table.reshape(peer_count, BCAP, 26), peer_ids)
    (face_grad, conv_total), interior = lax.scan(backward_step, start, xs)
    grad_conv = conv_total.reshape(27, channels, channels)
    grad_bricks = add_faces(interior.reshape(BRICKS, 8, 8, 8, channels), face_grad.reshape(BRICKS, 6, 8, 8, channels))
    grad_input = grad_bricks.astype(jnp.bfloat16).reshape(BRICKS, 8, 8, 8 * channels)
    return (coarse.reshape(CBRICKS, 512, CC), grad_input, grad_conv, grad_down)
```

```python
import jax
import jax.numpy as jnp
from jax import lax
from jax.experimental import pallas as pl
from jax.experimental.pallas import tpu as pltpu
from jax.sharding import PartitionSpec as P

MESH = pl.DeviceIdType.MESH
N_GRP, N_SUB = 8, 16
PEERS = N_GRP * N_SUB
NEAR = 33
C = 64
F32, BF16 = jnp.float32, jnp.bfloat16
LOCAL = 24
DUMP = LOCAL + 4 * NEAR
TABLE = DUMP + 4
VMEM_LIMIT = 50 * 1024 * 1024

OFFSETS = [
    (x, y, z)
    for x in (-1, 0, 1)
    for y in (-1, 0, 1)
    for z in (-1, 0, 1)
    if (x, y, z) != (0, 0, 0)
]
NUMBER = {offset: number for number, offset in enumerate(OFFSETS)}


def step_of(j):
    return jnp.where(j < 16, j + 1, jnp.where(j < 32, PEERS + 15 - j, 64))


def twin(j):
    return jnp.where(j < 16, j + 16, jnp.where(j < 32, j - 16, 32))


def coords(device):
    return (device // N_SUB, device % N_SUB)


def lane_iota(rows):
    return lax.broadcasted_iota(jnp.int32, (rows, 128), 1)


def row_iota(rows):
    return lax.broadcasted_iota(jnp.int32, (rows, 128), 0)


def half(tile):
    return pltpu.roll(tile, 64, axis=1)


def lows(rows):
    return lane_iota(rows) < 64


def to_face(tiles):
    top = jnp.concatenate([tiles[0], tiles[1]], axis=1)
    bottom = jnp.concatenate([tiles[2], tiles[3]], axis=1)
    return jnp.concatenate([top, bottom], axis=0)


def from_face(face):
    face = face.astype(F32)
    return [face[0:8, 0:128], face[0:8, 128:256], face[8:16, 0:128], face[8:16, 128:256]]


def exchange_kernel(
    feat, cot, dw, send, child,
    table, tg_out, place_out,
    flat, faces, sbuf, key_s, key_r, dwp, tg_s, tg_r,
    face_s, face_r, keys_s, keys_r, tgs_s, tgs_r, own_sem,
):
    grp, sub = lax.axis_index("grp"), lax.axis_index("sub")
    me = grp * N_SUB + sub
    barrier = pltpu.get_barrier_semaphore()

    def greet(j, _):
        peer = coords(lax.rem(me + step_of(j), PEERS))
        pl.semaphore_signal(barrier, inc=1, device_id=peer, device_id_type=MESH)
        return 0

    lax.fori_loop(0, NEAR, greet, 0)

    low = lows(8)
    for b in range(4):
        for x in range(8):
            v = feat[b, x].astype(F32)
            for q in range(4):
                flat[q * 256 + b * 64 + x * 8 : q * 256 + b * 64 + x * 8 + 8, :] = v[:, 128 * q : 128 * q + 128]

    def rows(q, b, y):
        return flat[pl.ds(q * 256 + b * 64 + y, 8, stride=8), :]

    for b in range(4):
        for s, x in ((0, 0), (1, 7)):
            v = feat[b, x].astype(F32)
            faces[b * 6 + s] = to_face([v[:, 128 * q : 128 * q + 128] for q in range(4)]).astype(BF16)
        for s, y in ((2, 0), (3, 7)):
            faces[b * 6 + s] = to_face([rows(q, b, y) for q in range(4)]).astype(BF16)
        first = [rows(0, b, y) for y in range(8)]
        last = [rows(3, b, y) for y in range(8)]
        faces[b * 6 + 4] = to_face(
            [jnp.where(low, first[2 * q], half(first[2 * q + 1])) for q in range(4)]
        ).astype(BF16)
        faces[b * 6 + 5] = to_face(
            [jnp.where(low, half(last[2 * q]), last[2 * q + 1]) for q in range(4)]
        ).astype(BF16)
    for i in range(4):
        faces[LOCAL + i] = jnp.zeros((16, 256), BF16)

    def pack(j, _):
        peer = lax.rem(me + step_of(j), PEERS)
        for k in range(4):
            code = send[peer * 4 + k]
            sbuf[j, k] = faces[jnp.maximum(code, 0)]
        return 0

    lax.fori_loop(0, NEAR, pack, 0)

    ijk = row_iota(8)
    for b in range(4):
        key_s[8 * b : 8 * b + 8] = (child[b] * 8 + ijk).astype(F32)
    key_r[sub] = key_s[...]

    pl.semaphore_wait(barrier, NEAR)

    def key_copy(s):
        other = lax.rem(sub + s, N_SUB)
        return pltpu.make_async_remote_copy(
            src_ref=key_s, dst_ref=key_r.at[sub], send_sem=keys_s.at[other], recv_sem=keys_r.at[sub],
            device_id=(grp, other), device_id_type=MESH,
        )

    def face_copy(j):
        return pltpu.make_async_remote_copy(
            src_ref=sbuf.at[j], dst_ref=table.at[pl.ds(LOCAL + 4 * twin(j), 4)],
            send_sem=face_s.at[j], recv_sem=face_r.at[twin(j)],
            device_id=coords(lax.rem(me + step_of(j), PEERS)), device_id_type=MESH,
        )

    def face_arrival(j):
        return pltpu.make_async_remote_copy(
            src_ref=sbuf.at[j], dst_ref=table.at[pl.ds(LOCAL + 4 * j, 4)],
            send_sem=face_s.at[j], recv_sem=face_r.at[j],
            device_id=coords(lax.rem(me + step_of(j), PEERS)), device_id_type=MESH,
        )

    def key_arrival(s):
        other = lax.rem(sub + s, N_SUB)
        return pltpu.make_async_remote_copy(
            src_ref=key_s, dst_ref=key_r.at[other], send_sem=keys_s.at[other], recv_sem=keys_r.at[other],
            device_id=(grp, other), device_id_type=MESH,
        )

    def tg_copy(s, arrival):
        other = lax.rem(sub + s, N_SUB)
        slot = other if arrival else sub
        return pltpu.make_async_remote_copy(
            src_ref=tg_s.at[other], dst_ref=tg_r.at[slot], send_sem=tgs_s.at[other], recv_sem=tgs_r.at[slot],
            device_id=(grp, other), device_id_type=MESH,
        )

    def loop(count, body, start=0):
        def step(i, _):
            body(i)
            return 0

        lax.fori_loop(start, count, step, 0)

    loop(N_SUB, lambda s: key_copy(s).start(), 1)
    loop(NEAR, lambda j: face_copy(j).start())
    own = [
        pltpu.make_async_copy(faces.at[pl.ds(0, LOCAL)], table.at[pl.ds(0, LOCAL)], own_sem.at[0]),
        pltpu.make_async_copy(faces.at[pl.ds(LOCAL, 4)], table.at[pl.ds(DUMP, 4)], own_sem.at[1]),
    ]
    for copy in own:
        copy.start()

    dwp[0:64] = dw[...]
    dwp[64:128] = dw[...]
    coarse_grad = lax.dot_general(
        cot[...], dwp[...], (((1,), (1,)), ((), ())), preferred_element_type=F32
    ).astype(BF16)

    def voxel_key(shape, dim):
        v = lax.broadcasted_iota(jnp.int32, shape, dim)
        x, y, z = v >> 6, (v >> 3) & 7, v & 7
        spot = 16 * (x >> 1) + 4 * (y >> 1) + (z >> 1)
        inner = 4 * (x & 1) + 2 * (y & 1) + (z & 1)
        return ((64 * sub + spot) * 8 + inner).astype(F32)

    loop(N_SUB, lambda s: key_arrival(s).wait_recv(), 1)
    keys = key_r[...].reshape(512, 128)
    wanted = jnp.broadcast_to(voxel_key((1, 512), 1), (512, 512))
    held = jnp.concatenate([keys] * 4, axis=1)
    take = jnp.where(held == wanted, 1.0, 0.0).astype(BF16)
    tiles = jnp.dot(take, coarse_grad, preferred_element_type=F32).astype(BF16)
    tg_s[...] = tiles.reshape(N_SUB, 32, 128)
    tg_r[sub] = tg_s[sub]
    loop(N_SUB, lambda s: tg_copy(s, False).start(), 1)
    key_row = jnp.concatenate([keys[128 * q : 128 * q + 128].T for q in range(4)], axis=1)[0:1]
    place_out[...] = jnp.where(
        jnp.broadcast_to(key_row, (512, 512)) == jnp.broadcast_to(voxel_key((512, 1), 0), (512, 512)), 1.0, 0.0
    ).astype(BF16)
    loop(N_SUB, lambda s: tg_copy(s, True).wait_recv(), 1)
    total = tg_r[0].astype(F32)
    for s in range(1, N_SUB):
        total += tg_r[s].astype(F32)
    tg_out[...] = total
    for copy in own:
        copy.wait()
    loop(NEAR, lambda j: face_arrival(j).wait_recv())
    loop(N_SUB, lambda s: key_copy(s).wait_send(), 1)
    loop(N_SUB, lambda s: tg_copy(s, False).wait_send(), 1)
    loop(NEAR, lambda j: face_copy(j).wait_send())


def widen(tiles, below, above):
    low = lows(tiles[0].shape[0])
    rolled = [half(tile) for tile in tiles]
    result = [jnp.where(low, half(below), rolled[0])]
    for m in range(1, 4):
        result.append(jnp.where(low, rolled[m - 1], rolled[m]))
    result.append(jnp.where(low, rolled[3], half(above)))
    return result


def narrow(tiles):
    low = lows(tiles[0].shape[0])
    rolled = [half(tile) for tile in tiles]
    return [jnp.where(low, rolled[q], rolled[q + 1]) for q in range(4)]


def roll8(value, shift):
    rows = value.shape[0]
    grouped = value.reshape(rows // 8, 8, 128)
    return pltpu.roll(grouped, shift % 8, axis=1).reshape(rows, 128)


def compute_kernel(
    table, tg, feat, cw, idx,
    tile_out, conv_out, back_out, faces_out, inner_out,
    band, bandt, zrim, yrim, pad, pre, pg, pgt, acc_a, acc,
):
    low8, row8 = lows(8), row_iota(8)
    zeros8 = jnp.zeros((8, 128), F32)

    band[...] = jnp.zeros_like(band)
    bandt[...] = jnp.zeros_like(bandt)
    for n in range(9):
        for s in range(3):
            w = cw[3 * n + s]
            band[n, 64 * s : 64 * s + 64, 0:64] = w
            band[n, 64 * s + 64 : 64 * s + 128, 64:128] = w
            d = 2 - s
            bandt[n, 0:64, 64 * d : 64 * d + 64] = w
            bandt[n, 64:128, 64 * d + 64 : 64 * d + 128] = w

    def slab(b, offset):
        return from_face(table[idx[b, NUMBER[offset]]])

    for b in range(4):
        below, above = slab(b, (0, 0, -1)), slab(b, (0, 0, 1))
        for y in range(8):
            q = y // 2
            if y % 2 == 0:
                value = jnp.where(low8, above[q], half(below[q]))
            else:
                value = jnp.where(low8, half(above[q]), below[q])
            zrim[pl.ds(b * 8 + y, 8, stride=32), :] = value
        for dy, row in ((-1, 7), (1, 0)):
            wide = widen(slab(b, (0, dy, 0)), slab(b, (0, dy, -1))[3], slab(b, (0, dy, 1))[0])
            for m in range(5):
                yrim[pl.ds(m * 256 + b * 8 + row, 8, stride=32), :] = wide[m]

    def put(m, first, value, before, after):
        rows = value.shape[0]
        lanes = slice(128 * m, 128 * m + 128)
        row = row_iota(rows) & 7
        pad[1, first : first + rows, lanes] = value.astype(BF16)
        pad[0, first : first + rows, lanes] = roll8(jnp.where(row == 7, before, value), 1).astype(BF16)
        pad[2, first : first + rows, lanes] = roll8(jnp.where(row == 0, after, value), -1).astype(BF16)

    for side, dx, plane in ((0, -1, 0), (1, 1, 9)):
        parts = [[], [], []]
        for b in range(4):
            for i, dy in enumerate((-1, 0, 1)):
                parts[i].append(
                    widen(slab(b, (dx, dy, 0)), slab(b, (dx, dy, -1))[3], slab(b, (dx, dy, 1))[0])
                )
        for m in range(5):
            before, value, after = [
                jnp.concatenate([part[b][m] for b in range(4)], axis=0) for part in parts
            ]
            put(m, plane * 32, value, before, after)
    for x in range(8):
        inner = []
        for q in range(4):
            inner.append(
                jnp.concatenate([feat[b, x][:, 128 * q : 128 * q + 128].astype(F32) for b in range(4)], axis=0)
            )
        rim = zrim[32 * x : 32 * x + 32, :]
        wide = widen(inner, rim, rim)
        for m in range(5):
            edge = yrim[m * 256 + 32 * x : m * 256 + 32 * x + 32, :]
            put(m, 32 * x + 32, wide[m], edge, edge)

    for m in range(4):
        total = None
        for n in range(9):
            sx, sy = n // 3, n % 3
            product = jnp.dot(
                pad[sy, 32 * sx : 32 * sx + 256, 128 * m : 128 * m + 256], band[n], preferred_element_type=F32
            )
            total = product if total is None else total + product
        pre[256 * m : 256 * m + 256] = total

    pg[...] = jnp.zeros_like(pg)
    grad = tg[...].reshape(4, 8, 128)
    sub_row = lax.broadcasted_iota(jnp.int32, (4, 8, 128), 1)
    pooled = jnp.zeros((4, 8, 128), F32)
    for top in range(2):
        for deep in range(2):
            spread = jnp.where(
                sub_row < 4,
                jnp.broadcast_to(grad[:, 4 * top + deep : 4 * top + deep + 1, :], (4, 8, 128)),
                jnp.broadcast_to(grad[:, 4 * top + 2 + deep : 4 * top + 3 + deep, :], (4, 8, 128)),
            ).reshape(32, 128) * (1.0 / 64.0)
            total = jnp.zeros((32, 128), F32)
            for m in (2 * deep, 2 * deep + 1):
                for x in range(4 * top, 4 * top + 4):
                    u = pre[256 * m + 32 * x : 256 * m + 32 * x + 32, :]
                    g = 1.0 / (1.0 + jnp.exp(-u))
                    total += u * g
                    slope = g * (1.0 + u * (1.0 - g))
                    pg[64 + 32 * x : 96 + 32 * x, 128 * m + 128 : 128 * m + 256] = (spread * slope).astype(BF16)
            total = total + half(total)
            grouped = total.reshape(4, 8, 128)
            grouped = grouped + pltpu.roll(grouped, 7, axis=1)
            grouped = grouped + pltpu.roll(grouped, 6, axis=1)
            for mid in range(2):
                pooled = jnp.where(
                    sub_row == 4 * top + 2 * mid + deep,
                    jnp.broadcast_to(grouped[:, 4 * mid : 4 * mid + 1, :], (4, 8, 128)),
                    pooled,
                )
    pooled = pooled.reshape(32, 128) * (1.0 / 64.0)
    tile_out[...] = jnp.where(lows(32), pooled, 0.0).astype(BF16)

    for m in range(4):
        pgt[:, 256 * m : 256 * m + 256] = (
            pg[64:320, 128 * m + 128 : 128 * m + 256].astype(F32).T.astype(BF16)
        )
    low64 = lows(64)
    held = None
    for n in range(9):
        sx, sy = n // 3, n % 3
        total = None
        for m in range(4):
            product = jnp.dot(
                pgt[:, 256 * m : 256 * m + 256],
                pad[sy, 32 * sx : 32 * sx + 256, 128 * m : 128 * m + 256],
                preferred_element_type=F32,
            )
            total = product if total is None else total + product
        r0, r1 = half(total[64:128, 0:128]), half(total[64:128, 128:256])
        first = total[0:64, 0:128] + jnp.where(low64, r0, r1)
        second = total[0:64, 128:256] + r1
        at = 3 * (n // 2)
        if n % 2 == 0:
            conv_out[at] = first
            held = second
        else:
            turned = half(first)
            conv_out[at + 1] = jnp.where(low64, held, turned)
            conv_out[at + 2] = jnp.where(low64, turned, half(second))
    conv_out[13] = jnp.where(low64, held, 0.0)
    conv_out[14] = jnp.zeros((64, 128), F32)
    conv_out[15] = jnp.zeros((64, 128), F32)

    for sy in range(3):
        for m in range(5):
            total = None
            for sx in range(3):
                product = lax.dot_general(
                    pg[32 * (2 - sx) : 32 * (2 - sx) + 320, 128 * m : 128 * m + 256],
                    bandt[3 * sx + sy],
                    (((1,), (1,)), ((), ())),
                    preferred_element_type=F32,
                )
                total = product if total is None else total + product
            acc_a[(sy * 5 + m) * 320 : (sy * 5 + m) * 320 + 320, :] = total

    def part(sy, m, first, rows):
        return acc_a[(sy * 5 + m) * 320 + first : (sy * 5 + m) * 320 + first + rows, :]

    def middle(m, first, rows):
        row = row_iota(rows) & 7
        return (
            part(1, m, first, rows)
            + jnp.where(row < 7, roll8(part(0, m, first, rows), -1), 0.0)
            + jnp.where(row > 0, roll8(part(2, m, first, rows), 1), 0.0)
        )

    acc[...] = jnp.zeros_like(acc)

    def add(b, offset, tiles):
        code = idx[b, NUMBER[offset]]
        for q, tile in enumerate(tiles):
            if tile is not None:
                acc[code, :, 128 * q : 128 * q + 128] += tile

    for x in range(8):
        wide = [middle(m, 32 * x + 32, 32) for m in range(5)]
        for q, tile in enumerate(narrow(wide)):
            inner_out[256 * q + 32 * x : 256 * q + 32 * x + 32, :] = tile
        zrim[32 * x : 32 * x + 32, :] = jnp.where(lows(32), wide[0], wide[4])

    for side, dx, plane in ((0, -1, 0), (1, 1, 9)):
        for b in range(4):
            first = 32 * plane + 8 * b
            rims = (
                (0, [middle(m, first, 8) for m in range(5)]),
                (-1, [jnp.where(row8 == 7, roll8(part(0, m, first, 8), -1), 0.0) for m in range(5)]),
                (1, [jnp.where(row8 == 0, roll8(part(2, m, first, 8), 1), 0.0) for m in range(5)]),
            )
            for dy, wide in rims:
                add(b, (dx, dy, 0), narrow(wide))
                add(b, (dx, dy, 1), [jnp.where(low8, half(wide[4]), 0.0), None, None, None])
                add(b, (dx, dy, -1), [None, None, None, jnp.where(low8, 0.0, half(wide[0]))])
    for b in range(4):
        for dy, sy, row in ((-1, 0, 0), (1, 2, 7)):
            wide = [
                acc_a[pl.ds((sy * 5 + m) * 320 + 32 + b * 8 + row, 8, stride=32), :] for m in range(5)
            ]
            add(b, (0, dy, 0), narrow(wide))
            add(b, (0, dy, 1), [jnp.where(low8, half(wide[4]), 0.0), None, None, None])
            add(b, (0, dy, -1), [None, None, None, jnp.where(low8, 0.0, half(wide[0]))])
        rims = [zrim[pl.ds(b * 8 + y, 8, stride=32), :] for y in range(8)]
        add(b, (0, 0, -1), [jnp.where(low8, rims[2 * q], half(rims[2 * q + 1])) for q in range(4)])
        add(b, (0, 0, 1), [jnp.where(low8, half(rims[2 * q]), rims[2 * q + 1]) for q in range(4)])

    faces_out[...] = acc[0:LOCAL]

    def leave(j, _):
        for k in range(4):
            value = acc[LOCAL + 4 * j + k]
            back_out[j, 16 * k : 16 * k + 16] = to_face(
                [value[:, 128 * q : 128 * q + 128] for q in range(4)]
            ).astype(BF16)
        return 0

    lax.fori_loop(0, NEAR, leave, 0)


def reduce_kernel(
    back, tiles, place, cot, dw, conv,
    returned, coarse_out, sums,
    tile_r, dwp, rs1, rs2, total1, fin,
    face_s, face_r, tile_ss, tile_rs, one_s, one_r, two_s, two_r, three_s, three_r, four_s, four_r, own_sem,
):
    grp, sub = lax.axis_index("grp"), lax.axis_index("sub")
    me = grp * N_SUB + sub
    barrier = pltpu.get_barrier_semaphore()

    def loop(count, body, start=0):
        def step(i, _):
            body(i)
            return 0

        lax.fori_loop(start, count, step, 0)

    def signal(peer):
        pl.semaphore_signal(barrier, inc=1, device_id=peer, device_id_type=MESH)

    loop(NEAR, lambda j: signal(coords(lax.rem(me + step_of(j), PEERS))))
    for far in (2, 3, 5, 6):
        signal((lax.rem(grp + far, N_GRP), sub))
    tile_r[sub] = tiles[...]
    dwp[0:64] = dw[...]
    dwp[64:128] = jnp.zeros((64, 128), BF16)
    pl.semaphore_wait(barrier, NEAR + 4)

    def sub_copy(s, src, dst, send_sem, recv_sem, arrival):
        other = lax.rem(sub + s, N_SUB)
        slot = other if arrival else sub
        return pltpu.make_async_remote_copy(
            src_ref=src(other), dst_ref=dst.at[slot], send_sem=send_sem.at[other], recv_sem=recv_sem.at[slot],
            device_id=(grp, other), device_id_type=MESH,
        )

    def grp_copy(s, src, dst, send_sem, recv_sem, arrival):
        other = lax.rem(grp + s, N_GRP)
        slot = other if arrival else grp
        return pltpu.make_async_remote_copy(
            src_ref=src(other), dst_ref=dst(slot), send_sem=send_sem.at[other], recv_sem=recv_sem.at[slot],
            device_id=(other, sub), device_id_type=MESH,
        )

    def tile_copy(s, arrival):
        return sub_copy(s, lambda other: tiles, tile_r, tile_ss, tile_rs, arrival)

    def first_copy(s, arrival):
        return sub_copy(s, lambda other: conv.at[other], rs1, one_s, one_r, arrival)

    def second_copy(s, arrival):
        return grp_copy(
            s, lambda other: total1.at[pl.ds(8 * other, 8)], lambda slot: rs2.at[slot], two_s, two_r, arrival
        )

    def third_copy(s, arrival):
        return grp_copy(
            s, lambda other: fin.at[pl.ds(8 * grp, 8)], lambda slot: fin.at[pl.ds(8 * slot, 8)], three_s, three_r, arrival
        )

    def fourth_copy(s, arrival):
        return sub_copy(s, lambda other: fin, sums, four_s, four_r, arrival)

    def back_copy(j, arrival):
        slot = j if arrival else twin(j)
        return pltpu.make_async_remote_copy(
            src_ref=back.at[j], dst_ref=returned.at[slot], send_sem=face_s.at[j], recv_sem=face_r.at[slot],
            device_id=coords(lax.rem(me + step_of(j), PEERS)), device_id_type=MESH,
        )

    loop(N_SUB, lambda s: tile_copy(s, False).start(), 1)

    def first_start(s):
        @pl.when(lax.rem(sub + s, N_SUB) != 14)
        def _():
            first_copy(s, False).start()

    loop(N_SUB, first_start, 1)
    loop(NEAR, lambda j: back_copy(j, False).start())

    loop(N_SUB, lambda s: tile_copy(s, True).wait_recv(), 1)
    coarse_in = jnp.dot(place[...], tile_r[...].reshape(512, 128), preferred_element_type=F32)
    coarse_out[...] = jnp.dot(coarse_in.astype(BF16), dwp[...], preferred_element_type=F32).astype(BF16)
    down = jnp.dot(coarse_in.T.astype(BF16), cot[...], preferred_element_type=F32)
    down_ref = conv.at[14]
    rs1[sub] = conv[sub]

    return_down = down[0:64]
    total1[...] = return_down
    down_copy = pltpu.make_async_remote_copy(
        src_ref=total1, dst_ref=rs1.at[sub], send_sem=one_s.at[14], recv_sem=one_r.at[sub],
        device_id=(grp, 14), device_id_type=MESH,
    )

    @pl.when(sub != 14)
    def _():
        down_copy.start()

    @pl.when(sub == 14)
    def _():
        rs1[14] = total1[...]

    loop(N_SUB, lambda s: first_copy(s, True).wait_recv(), 1)

    @pl.when(sub != 14)
    def _():
        down_copy.wait_send()

    total = rs1[0]
    for s in range(1, N_SUB):
        total += rs1[s]
    total1[...] = total
    loop(N_GRP, lambda s: second_copy(s, False).start(), 1)
    rs2[grp] = total1[pl.ds(pl.multiple_of(8 * grp, 8), 8), :]
    loop(N_GRP, lambda s: second_copy(s, True).wait_recv(), 1)
    total = rs2[0]
    for s in range(1, N_GRP):
        total += rs2[s]
    fin[pl.ds(pl.multiple_of(8 * grp, 8), 8), :] = total
    loop(N_GRP, lambda s: third_copy(s, False).start(), 1)
    loop(N_GRP, lambda s: third_copy(s, True).wait_recv(), 1)
    own = pltpu.make_async_copy(fin, sums.at[sub], own_sem)
    own.start()
    loop(N_SUB, lambda s: fourth_copy(s, False).start(), 1)
    loop(NEAR, lambda j: back_copy(j, True).wait_recv())
    loop(N_SUB, lambda s: fourth_copy(s, True).wait_recv(), 1)
    own.wait()

    loop(N_SUB, lambda s: tile_copy(s, False).wait_send(), 1)

    def first_end(s):
        @pl.when(lax.rem(sub + s, N_SUB) != 14)
        def _():
            first_copy(s, False).wait_send()

    loop(N_SUB, first_end, 1)
    loop(N_GRP, lambda s: second_copy(s, False).wait_send(), 1)
    loop(N_GRP, lambda s: third_copy(s, False).wait_send(), 1)
    loop(N_SUB, lambda s: fourth_copy(s, False).wait_send(), 1)
    loop(NEAR, lambda j: back_copy(j, False).wait_send())


def finish_kernel(returned, faces, inner, sums, codes, grad_out, conv_out, down_out, acc, yrim, zrim):
    acc[0:LOCAL] = faces[...]

    def add(j, _):
        for k in range(4):
            code = codes[j, k]
            spot = jnp.where(code < 0, LOCAL, code)
            for q, tile in enumerate(from_face(returned[j, 16 * k : 16 * k + 16])):
                acc[spot, :, 128 * q : 128 * q + 128] += tile
        return 0

    lax.fori_loop(0, NEAR, add, 0)
    low8 = lows(8)
    for b in range(4):
        for face, row in ((2, 0), (3, 7)):
            for q in range(4):
                yrim[pl.ds(q * 256 + b * 8 + row, 8, stride=32), :] = acc[6 * b + face, :, 128 * q : 128 * q + 128]
        for y in range(8):
            lanes = slice(128 * (y // 2), 128 * (y // 2) + 128)
            below, above = acc[6 * b + 4, :, lanes], acc[6 * b + 5, :, lanes]
            if y % 2 == 0:
                value = jnp.where(low8, below, half(above))
            else:
                value = jnp.where(low8, half(below), above)
            zrim[pl.ds(b * 8 + y, 8, stride=32), :] = value
    row = row_iota(8)
    edge = jnp.logical_or(row == 0, row == 7)
    for b in range(4):
        for x in range(8):
            at = 32 * x + 8 * b
            rim = zrim[at : at + 8, :]
            tiles = []
            for q in range(4):
                value = inner[256 * q + at : 256 * q + at + 8, :]
                if x == 0 or x == 7:
                    value = value + acc[6 * b + (0 if x == 0 else 1), :, 128 * q : 128 * q + 128]
                value = value + jnp.where(edge, yrim[256 * q + at : 256 * q + at + 8, :], 0.0)
                if q == 0:
                    value = value + jnp.where(low8, rim, 0.0)
                if q == 3:
                    value = value + jnp.where(low8, 0.0, rim)
                tiles.append(value)
            grad_out[b, x] = jnp.concatenate(tiles, axis=1).astype(BF16)
    for s in range(14):
        turned = sums[s].T
        conv_out[2 * s] = turned[0:64]
        if s < 13:
            conv_out[2 * s + 1] = turned[64:128]
    down_out[...] = sums[14]


def vmem():
    return pl.BlockSpec(memory_space=pltpu.VMEM)


def smem():
    return pl.BlockSpec(memory_space=pltpu.SMEM)


def hbm():
    return pl.BlockSpec(memory_space=pl.ANY)


def dma(*shape):
    return pltpu.SemaphoreType.DMA(shape)


def per_device(features, conv_weight, down_weight, cotangent, src_table, send_list, child_map):
    me = lax.axis_index("grp") * N_SUB + lax.axis_index("sub")
    send = send_list.reshape(PEERS * 4)
    cot = cotangent.reshape(512, 128)

    table, tile_grad, place = pl.pallas_call(
        exchange_kernel,
        out_shape=(
            jax.ShapeDtypeStruct((TABLE, 16, 256), BF16),
            jax.ShapeDtypeStruct((32, 128), F32),
            jax.ShapeDtypeStruct((512, 512), BF16),
        ),
        in_specs=[vmem(), vmem(), vmem(), smem(), smem()],
        out_specs=(hbm(), vmem(), vmem()),
        scratch_shapes=[
            pltpu.VMEM((1024, 128), F32),
            pltpu.VMEM((LOCAL + 4, 16, 256), BF16),
            pltpu.VMEM((NEAR, 4, 16, 256), BF16),
            pltpu.VMEM((32, 128), F32),
            pltpu.VMEM((N_SUB, 32, 128), F32),
            pltpu.VMEM((128, 128), BF16),
            pltpu.VMEM((N_SUB, 32, 128), BF16),
            pltpu.VMEM((N_SUB, 32, 128), BF16),
            dma(NEAR), dma(NEAR), dma(N_SUB), dma(N_SUB), dma(N_SUB), dma(N_SUB), dma(2),
        ],
        compiler_params=pltpu.CompilerParams(
            collective_id=0, has_side_effects=True, vmem_limit_bytes=VMEM_LIMIT
        ),
        name="exchange",
    )(features, cot, down_weight, send, child_map)

    remote = src_table - LOCAL
    distance = ((remote >> 2) - me) & (PEERS - 1)
    near = jnp.where(distance <= 16, distance - 1, jnp.where(distance >= 112, PEERS + 15 - distance, 32))
    index = jnp.where(
        src_table < 0, DUMP, jnp.where(src_table < LOCAL, src_table, LOCAL + 4 * near + (remote & 3))
    )
    tile, conv_part, back, faces, inner = pl.pallas_call(
        compute_kernel,
        out_shape=(
            jax.ShapeDtypeStruct((32, 128), BF16),
            jax.ShapeDtypeStruct((N_SUB, 64, 128), F32),
            jax.ShapeDtypeStruct((NEAR, 64, 256), BF16),
            jax.ShapeDtypeStruct((LOCAL, 8, 512), F32),
            jax.ShapeDtypeStruct((1024, 128), F32),
        ),
        in_specs=[vmem(), vmem(), vmem(), vmem(), smem()],
        out_specs=(vmem(),) * 5,
        scratch_shapes=[
            pltpu.VMEM((9, 256, 128), BF16),
            pltpu.VMEM((9, 128, 256), BF16),
            pltpu.VMEM((256, 128), F32),
            pltpu.VMEM((1280, 128), F32),
            pltpu.VMEM((3, 320, 640), BF16),
            pltpu.VMEM((1024, 128), F32),
            pltpu.VMEM((384, 768), BF16),
            pltpu.VMEM((128, 1024), BF16),
            pltpu.VMEM((15 * 320, 128), F32),
            pltpu.VMEM((TABLE, 8, 512), F32),
        ],
        compiler_params=pltpu.CompilerParams(vmem_limit_bytes=VMEM_LIMIT),
        name="compute",
    )(table, tile_grad, features, conv_weight, index)

    returned, coarse, sums = pl.pallas_call(
        reduce_kernel,
        out_shape=(
            jax.ShapeDtypeStruct((NEAR, 64, 256), BF16),
            jax.ShapeDtypeStruct((512, 128), BF16),
            jax.ShapeDtypeStruct((N_SUB, 64, 128), F32),
        ),
        in_specs=[vmem()] * 6,
        out_specs=(hbm(), vmem(), hbm()),
        scratch_shapes=[
            pltpu.VMEM((N_SUB, 32, 128), BF16),
            pltpu.VMEM((128, 128), BF16),
            pltpu.VMEM((N_SUB, 64, 128), F32),
            pltpu.VMEM((N_GRP, 8, 128), F32),
            pltpu.VMEM((64, 128), F32),
            pltpu.VMEM((64, 128), F32),
            dma(NEAR), dma(NEAR), dma(N_SUB), dma(N_SUB), dma(N_SUB), dma(N_SUB),
            dma(N_GRP), dma(N_GRP), dma(N_GRP), dma(N_GRP), dma(N_SUB), dma(N_SUB),
            pltpu.SemaphoreType.DMA,
        ],
        compiler_params=pltpu.CompilerParams(
            collective_id=1, has_side_effects=True, vmem_limit_bytes=VMEM_LIMIT
        ),
        name="reduce",
    )(back, tile, place, cot, down_weight, conv_part)

    order = jnp.arange(NEAR, dtype=jnp.int32)
    codes = send_list[0][lax.rem(me + step_of(order), PEERS)]
    grad_input, grad_conv, grad_down = pl.pallas_call(
        finish_kernel,
        out_shape=(
            jax.ShapeDtypeStruct((4, 8, 8, 512), BF16),
            jax.ShapeDtypeStruct((27, C, C), F32),
            jax.ShapeDtypeStruct((C, 128), F32),
        ),
        in_specs=[vmem(), vmem(), vmem(), vmem(), smem()],
        out_specs=(vmem(),) * 3,
        scratch_shapes=[
            pltpu.VMEM((LOCAL + 1, 8, 512), F32),
            pltpu.VMEM((1024, 128), F32),
            pltpu.VMEM((256, 128), F32),
        ],
        compiler_params=pltpu.CompilerParams(vmem_limit_bytes=VMEM_LIMIT),
        name="finish",
    )(returned, faces, inner, sums, codes)
    return coarse.reshape(1, 512, 128), grad_input, grad_conv, grad_down


def solution(mesh):
    both = ("grp", "sub")
    placed = (
        P(both, None, None, None),
        P(),
        P(),
        P(both, None, None),
        P(both, None),
        P(both, None, None),
        P(both),
    )
    return jax.shard_map(
        per_device,
        mesh=mesh,
        in_specs=placed,
        out_specs=(P(both, None, None), P(both, None, None, None), P(), P()),
        check_vma=False,
    )
```

```python
import jax
import jax.numpy as jnp
from jax import lax
from jax.experimental import pallas as pl
from jax.experimental.pallas import tpu as pltpu
from jax.sharding import PartitionSpec as P

MESH = pl.DeviceIdType.MESH
N_GRP, N_SUB = 8, 16
PEERS = N_GRP * N_SUB
NEAR = 33
C = 64
F32, BF16 = jnp.float32, jnp.bfloat16
LOCAL = 24
DUMP = LOCAL + 4 * NEAR
TABLE = DUMP + 4
VMEM_LIMIT = 58 * 1024 * 1024
TERMS = 4 * 26
SLOTS = 4 * NEAR

OFFSETS = [
    (x, y, z)
    for x in (-1, 0, 1)
    for y in (-1, 0, 1)
    for z in (-1, 0, 1)
    if (x, y, z) != (0, 0, 0)
]
NUMBER = {offset: number for number, offset in enumerate(OFFSETS)}


def step_of(j):
    return jnp.where(j < 16, j + 1, jnp.where(j == 16, 64, j + 95))


def twin(j):
    return NEAR - 1 - j


def near_of(step):
    return jnp.where(step <= 16, step - 1, jnp.where(step == 64, 16, step - 95))


def coords(device):
    return (device // N_SUB, device % N_SUB)


def lane_iota(rows):
    return lax.broadcasted_iota(jnp.int32, (rows, 128), 1)


def row_iota(rows):
    return lax.broadcasted_iota(jnp.int32, (rows, 128), 0)


def half(tile):
    return pltpu.roll(tile, 64, axis=1)


def lows(rows):
    return lane_iota(rows) < 64


def to_face(tiles):
    top = jnp.concatenate([tiles[0], tiles[1]], axis=1)
    bottom = jnp.concatenate([tiles[2], tiles[3]], axis=1)
    return jnp.concatenate([top, bottom], axis=0)


def from_face(face):
    face = face.astype(F32)
    return [face[0:8, 0:128], face[0:8, 128:256], face[8:16, 0:128], face[8:16, 128:256]]


def widen(tiles, below, above):
    low = lows(tiles[0].shape[0])
    rolled = [half(tile) for tile in tiles]
    result = [jnp.where(low, half(below), rolled[0])]
    for m in range(1, 4):
        result.append(jnp.where(low, rolled[m - 1], rolled[m]))
    result.append(jnp.where(low, rolled[3], half(above)))
    return result


def narrow(tiles):
    low = lows(tiles[0].shape[0])
    rolled = [half(tile) for tile in tiles]
    return [jnp.where(low, rolled[q], rolled[q + 1]) for q in range(4)]


def roll8(value, shift):
    rows = value.shape[0]
    grouped = value.reshape(rows // 8, 8, 128)
    return pltpu.roll(grouped, shift % 8, axis=1).reshape(rows, 128)

def loop(count, body, start=0):
    def step(i, _):
        body(i)
        return 0

    lax.fori_loop(start, count, step, 0)


def column_max(value):
    best = value[0:8]
    for i in range(1, 16):
        best = jnp.maximum(best, value[8 * i : 8 * i + 8])
    for shift in (4, 2, 1):
        best = jnp.maximum(best, pltpu.roll(best, shift, axis=0))
    return best


def index_tables(src_v, send_v, ids, me):
    whole = (128, 128)
    below = lax.broadcasted_iota(jnp.int32, whole, 0)
    along = lax.broadcasted_iota(jnp.int32, whole, 1)
    rows = [jnp.broadcast_to(src_v[b : b + 1, :], whole) for b in range(4)]
    columns = [row.T for row in rows]

    def pick(cases, none):
        best = None
        for match, value in cases:
            value = jnp.where(match, value, -1)
            best = value if best is None else jnp.maximum(best, value)
        best = column_max(best)
        return jnp.where(best < 0, none, best)[0:1]

    for b in range(4):
        cases = []
        for c in range(b + 1):
            match = jnp.logical_and(columns[c] == rows[b], columns[c] >= 0)
            if c == b:
                match = jnp.logical_and(match, below < along)
            cases.append((match, 26 * c + below))
        ids[b : b + 1, :] = pick(cases, TERMS)
    for k in range(4):
        code = jnp.where(along < NEAR, LOCAL + 4 * ((me + step_of(along)) & (PEERS - 1)) + k, -5)
        ids[4 + k : 5 + k, :] = pick([(columns[b] == code, 26 * b + below) for b in range(4)], TERMS)
    code = jnp.where(along < LOCAL, along, -5)
    ids[8:9, :] = pick([(columns[b] == code, 26 * b + below) for b in range(4)], TERMS)

    def number(device):
        return 4 * jnp.clip(near_of((device - me) & (PEERS - 1)), 0, NEAR - 1)

    columns = [jnp.broadcast_to(send_v[:, k : k + 1], whole) for k in range(4)]
    rows = [column.T for column in columns]
    first, second = number(below), number(along)
    for k in range(4):
        cases = []
        for c in range(4):
            match = jnp.logical_and(columns[c] == rows[k], columns[c] >= 0)
            cases.append((jnp.logical_and(match, first + c < second + k), first + c))
        ids[9 + k : 10 + k, :] = pick(cases, SLOTS)
    ids[13:14, :] = pick([(columns[c] == along, first + c) for c in range(4)], SLOTS)


def block_kernel(
    feat_h, cw_h, dw_h, cot_h, src_h, send_h, child_s,
    coarse_h, grad_h, conv_h, down_h,
    feat, cw, dw, cot, src_s, src_p, src_v, send_s, send_v, ids, ids_s,
    flat, faces, table, sbuf, returned, key_s, key_r, dwp, tg_s, tg_r, place,
    band, bandt, zrim, yrim, pad, pre, pg, pgt, acc_a, term, inner,
    tile_s, tile_r, convt, rs1, tot, rs2, fin, ag1, ag1b, ag2, chain,
    coarse, grad, conv_v, down_v,
    face_ss, face_rs, back_ss, back_rs, key_ss, key_rs, tg_ss, tg_rs, tile_ss, tile_rs,
    one_ss, one_rs, oneb_ss, oneb_rs, two_ss, two_rs, three_ss, three_rs, four_ss, four_rs, in_sem, out_sem,
):
    grp, sub = lax.axis_index("grp"), lax.axis_index("sub")
    me = grp * N_SUB + sub

    barrier = pltpu.get_barrier_semaphore()

    def signal(peer):
        pl.semaphore_signal(barrier, inc=1, device_id=peer, device_id_type=MESH)

    def near_peer(j):
        return coords(lax.rem(me + step_of(j), PEERS))

    loop(NEAR, lambda j: signal(near_peer(j)))
    for far in (2, 3, 5, 6):
        signal((lax.rem(grp + far, N_GRP), sub))

    loads = [
        pltpu.make_async_copy(source, target, in_sem.at[i])
        for i, (source, target) in enumerate(
            (
                (feat_h, feat), (send_h, send_s), (send_h, send_v), (cw_h, cw), (cot_h, cot), (dw_h, dw),
                (src_h, src_s), (src_h, src_p),
            )
        )
    ]
    for load in loads:
        load.start()
    loads[0].wait()

    low8, row8 = lows(8), row_iota(8)
    for b in range(4):
        for x in range(8):
            v = feat[b, x].astype(F32)
            for q in range(4):
                flat[q * 256 + b * 64 + x * 8 : q * 256 + b * 64 + x * 8 + 8, :] = v[:, 128 * q : 128 * q + 128]

    def rows(q, b, y):
        return flat[pl.ds(q * 256 + b * 64 + y, 8, stride=8), :]

    def face(number, tiles):
        value = to_face(tiles).astype(BF16)
        faces[number] = value
        table[number] = value

    for b in range(4):
        for s, x in ((0, 0), (1, 7)):
            v = feat[b, x].astype(F32)
            face(b * 6 + s, [v[:, 128 * q : 128 * q + 128] for q in range(4)])
        for s, y in ((2, 0), (3, 7)):
            face(b * 6 + s, [rows(q, b, y) for q in range(4)])
        first = [rows(0, b, y) for y in range(8)]
        last = [rows(3, b, y) for y in range(8)]
        face(b * 6 + 4, [jnp.where(low8, first[2 * q], half(first[2 * q + 1])) for q in range(4)])
        face(b * 6 + 5, [jnp.where(low8, half(last[2 * q]), last[2 * q + 1]) for q in range(4)])
    table[DUMP] = jnp.zeros((16, 256), BF16)
    for b in range(4):
        key_s[b : b + 1] = jnp.full((1, 128), 8 * child_s[b], jnp.int32)
    loads[1].wait()

    def pack(j):
        peer = lax.rem(me + step_of(j), PEERS)
        for k in range(4):
            sbuf[j, k] = faces[jnp.maximum(send_s[0, peer, k], 0)]

    loop(NEAR, pack)
    key_s[4:8] = jnp.zeros((4, 128), jnp.int32)
    key_r[sub] = key_s[...]
    pl.semaphore_wait(barrier, NEAR + 4)

    def sub_copy(s, src, dst, send_sem, recv_sem, arrival):
        other = lax.rem(sub + s, N_SUB)
        slot = other if arrival else sub
        return pltpu.make_async_remote_copy(
            src_ref=src(other), dst_ref=dst.at[slot], send_sem=send_sem.at[other], recv_sem=recv_sem.at[slot],
            device_id=(grp, other), device_id_type=MESH,
        )

    def grp_copy(s, src, dst, send_sem, recv_sem, arrival):
        other = lax.rem(grp + s, N_GRP)
        slot = other if arrival else grp
        return pltpu.make_async_remote_copy(
            src_ref=src(other), dst_ref=dst(slot), send_sem=send_sem.at[other], recv_sem=recv_sem.at[slot],
            device_id=(other, sub), device_id_type=MESH,
        )

    def near_copy(j, dst, send_sem, recv_sem, arrival):
        slot = j if arrival else twin(j)
        return pltpu.make_async_remote_copy(
            src_ref=sbuf.at[j], dst_ref=dst(slot), send_sem=send_sem.at[j], recv_sem=recv_sem.at[slot],
            device_id=near_peer(j), device_id_type=MESH,
        )

    def key_copy(s, arrival):
        return sub_copy(s, lambda other: key_s, key_r, key_ss, key_rs, arrival)

    def tg_copy(s, arrival):
        return sub_copy(s, lambda other: tg_s.at[other], tg_r, tg_ss, tg_rs, arrival)

    def tile_copy(s, arrival):
        return sub_copy(s, lambda other: tile_s, tile_r, tile_ss, tile_rs, arrival)

    def face_copy(j, arrival):
        return near_copy(j, lambda slot: table.at[pl.ds(LOCAL + 4 * slot, 4)], face_ss, face_rs, arrival)

    def back_copy(j, arrival):
        return near_copy(j, lambda slot: returned.at[slot], back_ss, back_rs, arrival)

    def one_copy(s, arrival):
        return grp_copy(
            s, lambda other: convt.at[other, pl.ds(0, 112)], lambda slot: rs1.at[slot, pl.ds(0, 112)],
            one_ss, one_rs, arrival,
        )

    def oneb_copy(s, arrival):
        return grp_copy(
            s, lambda other: convt.at[other, pl.ds(112, 16)], lambda slot: rs1.at[slot, pl.ds(112, 16)],
            oneb_ss, oneb_rs, arrival,
        )

    def two_copy(s, arrival):
        return sub_copy(s, lambda other: tot.at[pl.ds(8 * other, 8)], rs2, two_ss, two_rs, arrival)

    def three_copy(s, arrival):
        return sub_copy(s, lambda other: fin, ag1, three_ss, three_rs, arrival)

    def four_copy(s, arrival):
        return grp_copy(s, lambda other: ag1b, lambda slot: ag2.at[slot], four_ss, four_rs, arrival)

    loop(N_SUB, lambda s: key_copy(s, False).start(), 1)
    loop(NEAR, lambda j: face_copy(j, False).start())

    for load in loads[2:]:
        load.wait()
    band[...] = jnp.zeros_like(band)
    bandt[...] = jnp.zeros_like(bandt)
    for n in range(9):
        for s in range(3):
            w = cw[3 * n + s]
            band[n, 64 * s : 64 * s + 64, 0:64] = w
            band[n, 64 * s + 64 : 64 * s + 128, 64:128] = w
            d = 2 - s
            bandt[n, 0:64, 64 * d : 64 * d + 64] = w
            bandt[n, 64:128, 64 * d + 64 : 64 * d + 128] = w
    src_v[...] = jnp.full((8, 128), -1, jnp.int32)
    src_v[0:4, 0:26] = src_p[...]
    index_tables(src_v, send_v.at[0], ids, me)
    to_scalars = pltpu.make_async_copy(ids, ids_s, in_sem.at[8])
    to_scalars.start()
    pg[...] = jnp.zeros_like(pg)
    term[TERMS] = jnp.zeros((8, 512), F32)
    chain[SLOTS] = jnp.zeros((8, 512), F32)
    dwp[0:64] = dw[...]
    dwp[64:128] = dw[...]
    coarse_grad = lax.dot_general(
        cot[0], dwp[...], (((1,), (1,)), ((), ())), preferred_element_type=F32
    ).astype(BF16)

    def voxel_key(shape, dim):
        v = lax.broadcasted_iota(jnp.int32, shape, dim)
        x, y, z = v >> 6, (v >> 3) & 7, v & 7
        spot = 16 * (x >> 1) + 4 * (y >> 1) + (z >> 1)
        inside = 4 * (x & 1) + 2 * (y & 1) + (z & 1)
        return (64 * sub + spot) * 8 + inside

    loop(N_SUB, lambda s: key_copy(s, True).wait_recv(), 1)
    ijk = row_iota(8)
    keys = jnp.concatenate(
        [jnp.broadcast_to(key_r[s, b : b + 1, :], (8, 128)) + ijk for s in range(N_SUB) for b in range(4)], axis=0
    )
    wanted = jnp.broadcast_to(voxel_key((1, 512), 1), (512, 512))
    take = jnp.where(jnp.concatenate([keys] * 4, axis=1) == wanted, 1.0, 0.0).astype(BF16)
    tiles = jnp.dot(take, coarse_grad, preferred_element_type=F32).astype(BF16)
    tg_s[...] = tiles.reshape(N_SUB, 32, 128)
    tg_r[sub] = tg_s[sub]
    loop(N_SUB, lambda s: tg_copy(s, False).start(), 1)
    key_row = jnp.concatenate([keys[128 * q : 128 * q + 128].T for q in range(4)], axis=1)[0:1]
    place[...] = jnp.where(
        jnp.broadcast_to(key_row, (512, 512)) == jnp.broadcast_to(voxel_key((512, 1), 0), (512, 512)), 1.0, 0.0
    ).astype(BF16)
    to_scalars.wait()
    loop(NEAR, lambda j: face_copy(j, True).wait_recv())

    def slab(b, offset):
        code = src_s[b, NUMBER[offset]]
        remote = code - LOCAL
        spot = LOCAL + 4 * near_of(((remote >> 2) - me) & (PEERS - 1)) + (remote & 3)
        return from_face(table[jnp.where(code < 0, DUMP, jnp.where(code < LOCAL, code, spot))])

    for b in range(4):
        below, above = slab(b, (0, 0, -1)), slab(b, (0, 0, 1))
        for y in range(8):
            q = y // 2
            if y % 2 == 0:
                value = jnp.where(low8, above[q], half(below[q]))
            else:
                value = jnp.where(low8, half(above[q]), below[q])
            zrim[pl.ds(b * 8 + y, 8, stride=32), :] = value
        for dy, row in ((-1, 7), (1, 0)):
            wide = widen(slab(b, (0, dy, 0)), slab(b, (0, dy, -1))[3], slab(b, (0, dy, 1))[0])
            for m in range(5):
                yrim[pl.ds(m * 256 + b * 8 + row, 8, stride=32), :] = wide[m]

    def put(m, first, value, before, after):
        count = value.shape[0]
        lanes = slice(128 * m, 128 * m + 128)
        row = row_iota(count) & 7
        pad[1, first : first + count, lanes] = value.astype(BF16)
        pad[0, first : first + count, lanes] = roll8(jnp.where(row == 7, before, value), 1).astype(BF16)
        pad[2, first : first + count, lanes] = roll8(jnp.where(row == 0, after, value), -1).astype(BF16)

    for dx, plane in ((-1, 0), (1, 9)):
        parts = [[], [], []]
        for b in range(4):
            for i, dy in enumerate((-1, 0, 1)):
                parts[i].append(
                    widen(slab(b, (dx, dy, 0)), slab(b, (dx, dy, -1))[3], slab(b, (dx, dy, 1))[0])
                )
        for m in range(5):
            before, value, after = [
                jnp.concatenate([part[b][m] for b in range(4)], axis=0) for part in parts
            ]
            put(m, plane * 32, value, before, after)
    for x in range(8):
        inside = []
        for q in range(4):
            inside.append(
                jnp.concatenate([feat[b, x][:, 128 * q : 128 * q + 128].astype(F32) for b in range(4)], axis=0)
            )
        rim = zrim[32 * x : 32 * x + 32, :]
        wide = widen(inside, rim, rim)
        for m in range(5):
            edge = yrim[m * 256 + 32 * x : m * 256 + 32 * x + 32, :]
            put(m, 32 * x + 32, wide[m], edge, edge)

    for m in range(4):
        total = None
        for n in range(9):
            sx, sy = n // 3, n % 3
            product = jnp.dot(
                pad[sy, 32 * sx : 32 * sx + 256, 128 * m : 128 * m + 256], band[n], preferred_element_type=F32
            )
            total = product if total is None else total + product
        pre[256 * m : 256 * m + 256] = total

    loop(N_SUB, lambda s: tg_copy(s, True).wait_recv(), 1)
    grad_tile = tg_r[0].astype(F32)
    for s in range(1, N_SUB):
        grad_tile += tg_r[s].astype(F32)
    grad_tile = grad_tile.reshape(4, 8, 128)
    sub_row = lax.broadcasted_iota(jnp.int32, (4, 8, 128), 1)
    pooled = jnp.zeros((4, 8, 128), F32)
    for top in range(2):
        for deep in range(2):
            spread = jnp.where(
                sub_row < 4,
                jnp.broadcast_to(grad_tile[:, 4 * top + deep : 4 * top + deep + 1, :], (4, 8, 128)),
                jnp.broadcast_to(grad_tile[:, 4 * top + 2 + deep : 4 * top + 3 + deep, :], (4, 8, 128)),
            ).reshape(32, 128) * (1.0 / 64.0)
            total = jnp.zeros((32, 128), F32)
            for m in (2 * deep, 2 * deep + 1):
                for x in range(4 * top, 4 * top + 4):
                    u = pre[256 * m + 32 * x : 256 * m + 32 * x + 32, :]
                    g = 1.0 / (1.0 + jnp.exp(-u))
                    total += u * g
                    slope = g * (1.0 + u * (1.0 - g))
                    pg[64 + 32 * x : 96 + 32 * x, 128 * m + 128 : 128 * m + 256] = (spread * slope).astype(BF16)
            total = total + half(total)
            grouped = total.reshape(4, 8, 128)
            grouped = grouped + pltpu.roll(grouped, 7, axis=1)
            grouped = grouped + pltpu.roll(grouped, 6, axis=1)
            for mid in range(2):
                pooled = jnp.where(
                    sub_row == 4 * top + 2 * mid + deep,
                    jnp.broadcast_to(grouped[:, 4 * mid : 4 * mid + 1, :], (4, 8, 128)),
                    pooled,
                )
    pooled = pooled.reshape(32, 128) * (1.0 / 64.0)
    tile_s[...] = jnp.where(lows(32), pooled, 0.0).astype(BF16)
    tile_r[sub] = tile_s[...]
    loop(N_SUB, lambda s: tile_copy(s, False).start(), 1)

    for m in range(4):
        pgt[:, 256 * m : 256 * m + 256] = (
            pg[64:320, 128 * m + 128 : 128 * m + 256].astype(F32).T.astype(BF16)
        )
    low64 = lows(64)

    def keep(chunk, value):
        for g in range(N_GRP):
            convt[g, 8 * chunk : 8 * chunk + 8] = value[8 * g : 8 * g + 8]

    held = None
    for n in range(9):
        sx, sy = n // 3, n % 3
        total = None
        for m in range(4):
            product = jnp.dot(
                pgt[:, 256 * m : 256 * m + 256],
                pad[sy, 32 * sx : 32 * sx + 256, 128 * m : 128 * m + 256],
                preferred_element_type=F32,
            )
            total = product if total is None else total + product
        r0, r1 = half(total[64:128, 0:128]), half(total[64:128, 128:256])
        first = total[0:64, 0:128] + jnp.where(low64, r0, r1)
        second = total[0:64, 128:256] + r1
        at = 3 * (n // 2)
        if n % 2 == 0:
            keep(at, first)
            held = second
        else:
            turned = half(first)
            keep(at + 1, jnp.where(low64, held, turned))
            keep(at + 2, jnp.where(low64, turned, half(second)))
    keep(13, jnp.where(low64, held, 0.0))
    loop(N_GRP, lambda s: one_copy(s, False).start(), 1)

    for sy in range(3):
        for m in range(5):
            total = None
            for sx in range(3):
                product = lax.dot_general(
                    pg[32 * (2 - sx) : 32 * (2 - sx) + 320, 128 * m : 128 * m + 256],
                    bandt[3 * sx + sy],
                    (((1,), (1,)), ((), ())),
                    preferred_element_type=F32,
                )
                total = product if total is None else total + product
            acc_a[(sy * 5 + m) * 320 : (sy * 5 + m) * 320 + 320, :] = total

    def part(sy, m, first, count):
        return acc_a[(sy * 5 + m) * 320 + first : (sy * 5 + m) * 320 + first + count, :]

    def middle(m, first, count):
        row = row_iota(count) & 7
        return (
            part(1, m, first, count)
            + jnp.where(row < 7, roll8(part(0, m, first, count), -1), 0.0)
            + jnp.where(row > 0, roll8(part(2, m, first, count), 1), 0.0)
        )

    for x in range(8):
        wide = [middle(m, 32 * x + 32, 32) for m in range(5)]
        for q, tile in enumerate(narrow(wide)):
            inner[256 * q + 32 * x : 256 * q + 32 * x + 32, :] = tile
        zrim[32 * x : 32 * x + 32, :] = jnp.where(lows(32), wide[0], wide[4])

    planes = {}
    for dx, plane in ((-1, 0), (1, 9)):
        for b in range(4):
            first = 32 * plane + 8 * b
            planes[dx, 0, b] = [middle(m, first, 8) for m in range(5)]
            planes[dx, -1, b] = [
                jnp.where(row8 == 7, roll8(part(0, m, first, 8), -1), 0.0) for m in range(5)
            ]
            planes[dx, 1, b] = [
                jnp.where(row8 == 0, roll8(part(2, m, first, 8), 1), 0.0) for m in range(5)
            ]

    def rim(b, offset):
        dx, dy, dz = offset
        if dx == 0 and dy == 0:
            rims = [zrim[pl.ds(b * 8 + y, 8, stride=32), :] for y in range(8)]
            if dz < 0:
                return [jnp.where(low8, rims[2 * q], half(rims[2 * q + 1])) for q in range(4)]
            return [jnp.where(low8, half(rims[2 * q]), rims[2 * q + 1]) for q in range(4)]
        if dx != 0:
            wide = planes[dx, dy, b]
        else:
            sy, row = (0, 0) if dy < 0 else (2, 7)
            wide = [
                acc_a[pl.ds((sy * 5 + m) * 320 + 32 + b * 8 + row, 8, stride=32), :] for m in range(5)
            ]
        if dz == 0:
            return narrow(wide)
        if dz > 0:
            return [jnp.where(low8, half(wide[4]), 0.0), None, None, None]
        return [None, None, None, jnp.where(low8, 0.0, half(wide[0]))]

    for b in range(4):
        for t, offset in enumerate(OFFSETS):
            earlier = ids_s[b, t]
            for q, tile in enumerate(rim(b, offset)):
                value = term[earlier, :, 128 * q : 128 * q + 128]
                term[26 * b + t, :, 128 * q : 128 * q + 128] = value if tile is None else value + tile

    def leave(j):
        face_copy(j, False).wait_send()
        for k in range(4):
            value = term[ids_s[4 + k, j]]
            sbuf[j, k] = to_face([value[:, 128 * q : 128 * q + 128] for q in range(4)]).astype(BF16)
        back_copy(j, False).start()

    loop(NEAR, leave)

    loop(N_SUB, lambda s: tile_copy(s, True).wait_recv(), 1)
    coarse_in = jnp.dot(place[...], tile_r[...].reshape(512, 128), preferred_element_type=F32)
    dwp[64:128] = jnp.zeros((64, 128), BF16)
    down = jnp.dot(coarse_in.T.astype(BF16), cot[0], preferred_element_type=F32)
    for g in range(N_GRP):
        convt[g, 112:120] = down[8 * g : 8 * g + 8]
        convt[g, 120:128] = jnp.zeros((8, 128), F32)
    loop(N_GRP, lambda s: oneb_copy(s, False).start(), 1)
    coarse[0] = jnp.dot(coarse_in.astype(BF16), dwp[...], preferred_element_type=F32).astype(BF16)
    coarse_store = pltpu.make_async_copy(coarse, coarse_h, out_sem.at[0])
    coarse_store.start()
    rs1[grp] = convt[grp]

    def both_arrivals(s):
        one_copy(s, True).wait_recv()
        oneb_copy(s, True).wait_recv()

    loop(N_GRP, both_arrivals, 1)
    total = rs1[0]
    for g in range(1, N_GRP):
        total += rs1[g]
    tot[...] = total
    loop(N_SUB, lambda s: two_copy(s, False).start(), 1)
    rs2[sub] = tot[pl.ds(pl.multiple_of(8 * sub, 8), 8), :]
    loop(N_SUB, lambda s: two_copy(s, True).wait_recv(), 1)
    total = rs2[0]
    for s in range(1, N_SUB):
        total += rs2[s]
    fin[...] = total
    loop(N_SUB, lambda s: three_copy(s, False).start(), 1)
    ag1[sub] = fin[...]
    loop(N_SUB, lambda s: three_copy(s, True).wait_recv(), 1)
    ag1b[...] = ag1[...].reshape(128, 128).astype(BF16)
    loop(N_GRP, lambda s: four_copy(s, False).start(), 1)
    ag2[grp] = ag1b[...]

    def take_back(j):
        back_copy(j, True).wait_recv()
        peer = lax.rem(me + step_of(j), PEERS)
        for k in range(4):
            value = chain[ids_s[9 + k, peer]]
            tiles = from_face(returned[j, k])
            for q in range(4):
                chain[4 * j + k, :, 128 * q : 128 * q + 128] = value[:, 128 * q : 128 * q + 128] + tiles[q]

    loop(NEAR, take_back)

    face_sums = [term[ids_s[8, f]] + chain[ids_s[13, f]] for f in range(LOCAL)]

    def tile_of(f, q):
        return face_sums[f][:, 128 * q : 128 * q + 128]

    for b in range(4):
        for f, row in ((2, 0), (3, 7)):
            for q in range(4):
                yrim[pl.ds(q * 256 + b * 8 + row, 8, stride=32), :] = tile_of(6 * b + f, q)
        for y in range(8):
            below, above = tile_of(6 * b + 4, y // 2), tile_of(6 * b + 5, y // 2)
            if y % 2 == 0:
                value = jnp.where(low8, below, half(above))
            else:
                value = jnp.where(low8, half(below), above)
            zrim[pl.ds(b * 8 + y, 8, stride=32), :] = value
    edge = jnp.logical_or(row8 == 0, row8 == 7)
    for b in range(4):
        for x in range(8):
            at = 32 * x + 8 * b
            rim_z = zrim[at : at + 8, :]
            tiles = []
            for q in range(4):
                value = inner[256 * q + at : 256 * q + at + 8, :]
                if x == 0 or x == 7:
                    value = value + tile_of(6 * b + (0 if x == 0 else 1), q)
                value = value + jnp.where(edge, yrim[256 * q + at : 256 * q + at + 8, :], 0.0)
                if q == 0:
                    value = value + jnp.where(low8, rim_z, 0.0)
                if q == 3:
                    value = value + jnp.where(low8, 0.0, rim_z)
                tiles.append(value)
            grad[b, x] = jnp.concatenate(tiles, axis=1).astype(BF16)
    grad_store = pltpu.make_async_copy(grad, grad_h, out_sem.at[1])
    grad_store.start()

    loop(N_GRP, lambda s: four_copy(s, True).wait_recv(), 1)
    got = [ag2[g].astype(F32) for g in range(N_GRP)]
    for s in range(15):
        value = jnp.concatenate([got[g][8 * s : 8 * s + 8] for g in range(N_GRP)], axis=0)
        if s == 14:
            down_v[...] = value
        else:
            turned = value.T
            conv_v[2 * s] = turned[0:64]
            if s < 13:
                conv_v[2 * s + 1] = turned[64:128]
    conv_store = pltpu.make_async_copy(conv_v, conv_h, out_sem.at[2])
    conv_store.start()
    down_store = pltpu.make_async_copy(down_v, down_h, out_sem.at[3])
    down_store.start()

    def sub_ends(s):
        for copy in (key_copy, tg_copy, tile_copy, two_copy, three_copy):
            copy(s, False).wait_send()

    def grp_ends(s):
        for copy in (one_copy, oneb_copy, four_copy):
            copy(s, False).wait_send()

    loop(N_SUB, sub_ends, 1)
    loop(N_GRP, grp_ends, 1)
    loop(NEAR, lambda j: back_copy(j, False).wait_send())
    for store in (coarse_store, grad_store, conv_store, down_store):
        store.wait()


def dma(*shape):
    return pltpu.SemaphoreType.DMA(shape)


def per_device(features, conv_weight, down_weight, cotangent, src_table, send_list, child_map):
    hbm = pl.BlockSpec(memory_space=pl.ANY)
    vmem, smem, i32 = pltpu.VMEM, pltpu.SMEM, jnp.int32
    coarse, grad_input, grad_conv, grad_down = pl.pallas_call(
        block_kernel,
        out_shape=(
            jax.ShapeDtypeStruct((1, 512, 128), BF16),
            jax.ShapeDtypeStruct((4, 8, 8, 512), BF16),
            jax.ShapeDtypeStruct((27, C, C), F32),
            jax.ShapeDtypeStruct((C, 128), F32),
        ),
        in_specs=[hbm] * 6 + [pl.BlockSpec(memory_space=pltpu.SMEM)],
        out_specs=(hbm,) * 4,
        scratch_shapes=[
            vmem((4, 8, 8, 512), BF16), vmem((27, C, C), BF16), vmem((C, 128), BF16), vmem((1, 512, 128), BF16),
            smem((4, 26), i32), vmem((4, 26), i32), vmem((8, 128), i32),
            smem((1, PEERS, 4), i32), vmem((1, PEERS, 4), i32), vmem((16, 128), i32), smem((16, 128), i32),
            vmem((1024, 128), F32),
            vmem((LOCAL, 16, 256), BF16),
            vmem((TABLE, 16, 256), BF16),
            vmem((NEAR, 4, 16, 256), BF16),
            vmem((NEAR, 4, 16, 256), BF16),
            vmem((8, 128), i32), vmem((N_SUB, 8, 128), i32),
            vmem((128, 128), BF16),
            vmem((N_SUB, 32, 128), BF16), vmem((N_SUB, 32, 128), BF16),
            vmem((512, 512), BF16),
            vmem((9, 256, 128), BF16), vmem((9, 128, 256), BF16),
            vmem((256, 128), F32), vmem((1280, 128), F32),
            vmem((3, 320, 640), BF16),
            vmem((1024, 128), F32),
            vmem((384, 768), BF16),
            vmem((128, 1024), BF16),
            vmem((15 * 320, 128), F32),
            vmem((TERMS + 1, 8, 512), F32),
            vmem((1024, 128), F32),
            vmem((32, 128), BF16), vmem((N_SUB, 32, 128), BF16),
            vmem((N_GRP, 128, 128), F32), vmem((N_GRP, 128, 128), F32), vmem((128, 128), F32),
            vmem((N_SUB, 8, 128), F32), vmem((8, 128), F32), vmem((N_SUB, 8, 128), F32),
            vmem((128, 128), BF16), vmem((N_GRP, 128, 128), BF16),
            vmem((SLOTS + 1, 8, 512), F32),
            vmem((1, 512, 128), BF16), vmem((4, 8, 8, 512), BF16), vmem((27, C, C), F32), vmem((C, 128), F32),
        ]
        + [dma(NEAR)] * 4
        + [dma(N_SUB)] * 6
        + [dma(N_GRP)] * 4
        + [dma(N_SUB)] * 4
        + [dma(N_GRP)] * 2
        + [dma(9), dma(4)],
        compiler_params=pltpu.CompilerParams(
            collective_id=0, has_side_effects=True, vmem_limit_bytes=VMEM_LIMIT
        ),
        name="block",
    )(features, conv_weight, down_weight, cotangent, src_table, send_list, child_map)
    return coarse, grad_input, grad_conv, grad_down


def solution(mesh):
    both = ("grp", "sub")
    placed = (
        P(both, None, None, None),
        P(),
        P(),
        P(both, None, None),
        P(both, None),
        P(both, None, None),
        P(both),
    )
    return jax.shard_map(
        per_device,
        mesh=mesh,
        in_specs=placed,
        out_specs=(P(both, None, None), P(both, None, None, None), P(), P()),
        check_vma=False,
    )
```

```python
import jax
import jax.numpy as jnp
from jax import lax
from jax.experimental import pallas as pl
from jax.experimental.pallas import tpu as pltpu
from jax.sharding import PartitionSpec as P

LOGICAL = pl.DeviceIdType.LOGICAL
N_GRP, N_SUB = 8, 16
PEERS = N_GRP * N_SUB
NEAR = 33
C = 64
F32, BF16 = jnp.float32, jnp.bfloat16
LOCAL = 24
DUMP = LOCAL + 4 * NEAR
TABLE = DUMP + 4
VMEM_LIMIT = 58 * 1024 * 1024
TERMS = 4 * 26
FIRST_FACES = NEAR
SLOTS = 4 * NEAR

OFFSETS = [
    (x, y, z)
    for x in (-1, 0, 1)
    for y in (-1, 0, 1)
    for z in (-1, 0, 1)
    if (x, y, z) != (0, 0, 0)
]
NUMBER = {offset: number for number, offset in enumerate(OFFSETS)}


def step_of(j):
    return jnp.where(j < 16, j + 1, jnp.where(j == 16, 64, j + 95))


def twin(j):
    return NEAR - 1 - j


def near_of(step):
    return jnp.where(step <= 16, step - 1, jnp.where(step == 64, 16, step - 95))


def lane_iota(rows):
    return lax.broadcasted_iota(jnp.int32, (rows, 128), 1)


def row_iota(rows):
    return lax.broadcasted_iota(jnp.int32, (rows, 128), 0)


def half(tile):
    return pltpu.roll(tile, 64, axis=1)


def lows(rows):
    return lane_iota(rows) < 64


def to_face(tiles):
    top = jnp.concatenate([tiles[0], tiles[1]], axis=1)
    bottom = jnp.concatenate([tiles[2], tiles[3]], axis=1)
    return jnp.concatenate([top, bottom], axis=0)


def from_face(face):
    face = face.astype(F32)
    return [face[0:8, 0:128], face[0:8, 128:256], face[8:16, 0:128], face[8:16, 128:256]]


def widen(tiles, below, above):
    low = lows(tiles[0].shape[0])
    rolled = [half(tile) for tile in tiles]
    result = [jnp.where(low, half(below), rolled[0])]
    for m in range(1, 4):
        result.append(jnp.where(low, rolled[m - 1], rolled[m]))
    result.append(jnp.where(low, rolled[3], half(above)))
    return result


def narrow(tiles):
    low = lows(tiles[0].shape[0])
    rolled = [half(tile) for tile in tiles]
    return [jnp.where(low, rolled[q], rolled[q + 1]) for q in range(4)]


def roll8(value, shift):
    rows = value.shape[0]
    grouped = value.reshape(rows // 8, 8, 128)
    return pltpu.roll(grouped, shift % 8, axis=1).reshape(rows, 128)

def loop(count, body, start=0, unroll=True):
    def step(i, _):
        body(i)
        return 0

    lax.fori_loop(start, count, step, 0, unroll=unroll)


def column_max(value):
    best = value[0:8]
    for i in range(1, 16):
        best = jnp.maximum(best, value[8 * i : 8 * i + 8])
    for shift in (4, 2, 1):
        best = jnp.maximum(best, pltpu.roll(best, shift, axis=0))
    return best


def index_tables(src_v, send_v, ids, me):
    whole = (128, 128)
    below = lax.broadcasted_iota(jnp.int32, whole, 0)
    along = lax.broadcasted_iota(jnp.int32, whole, 1)
    rows = [jnp.broadcast_to(src_v[b : b + 1, :], whole) for b in range(4)]
    columns = [row.T for row in rows]

    def pick(cases, none):
        best = None
        for match, value in cases:
            value = jnp.where(match, value, -1)
            best = value if best is None else jnp.maximum(best, value)
        best = column_max(best)
        return jnp.where(best < 0, none, best)[0:1]

    for b in range(4):
        cases = []
        for c in range(b + 1):
            match = jnp.logical_and(columns[c] == rows[b], columns[c] >= 0)
            if c == b:
                match = jnp.logical_and(match, below < along)
            cases.append((match, 26 * c + below))
        ids[b : b + 1, :] = pick(cases, TERMS)
    for k in range(4):
        code = jnp.where(along < NEAR, LOCAL + 4 * ((me + step_of(along)) & (PEERS - 1)) + k, -5)
        ids[4 + k : 5 + k, :] = pick([(columns[b] == code, 26 * b + below) for b in range(4)], TERMS)
    code = jnp.where(along < LOCAL, along, -5)
    ids[8:9, :] = pick([(columns[b] == code, 26 * b + below) for b in range(4)], TERMS)

    def number(device):
        return 4 * jnp.clip(near_of((device - me) & (PEERS - 1)), 0, NEAR - 1)

    rows = [jnp.broadcast_to(send_v[k : k + 1, :], whole) for k in range(4)]
    columns = [row.T for row in rows]
    first, second = number(below), number(along)
    for k in range(4):
        cases = []
        for c in range(4):
            match = jnp.logical_and(columns[c] == rows[k], columns[c] >= 0)
            cases.append((jnp.logical_and(match, first + c < second + k), first + c))
        ids[9 + k : 10 + k, :] = pick(cases, SLOTS)
    ids[13:14, :] = pick([(columns[c] == along, first + c) for c in range(4)], SLOTS)


def block_kernel(
    feat_h, cw_h, dw_h, cot_h, src_h, send_h, child_s,
    coarse_h, grad_h, ag2,
    feat, cw, dw, cot, src_s, src_p, src_v, send_s, send_v, ids, ids_s,
    flat, faces, table, sbuf, returned, key_s, key_r, dwp, tg_s, tg_r, place,
    band, bandt, zrim, yrim, pad, pre, pg, pgt, acc_a, term, inner,
    tile_s, tile_r, convt, rs1, tot, rs2, fin, ag1, ag1b, chain, coarse, grad,
    face_sem, back_rs, key_sem, tg_sem, tile_sem, one_sem, two_sem, three_sem, four_sem, in_sem, out_sem,
):
    grp, sub = lax.axis_index("grp"), lax.axis_index("sub")
    me = grp * N_SUB + sub

    barrier = pltpu.get_barrier_semaphore()

    def signal(peer):
        pl.semaphore_signal(barrier, inc=1, device_id=peer, device_id_type=LOGICAL)

    def near_peer(j):
        return (me + step_of(j)) & (PEERS - 1)

    loop(NEAR, lambda j: signal(near_peer(j)))
    for far in (2, 3, 5, 6):
        signal(((grp + far) & (N_GRP - 1)) * N_SUB + sub)

    loads = [
        pltpu.make_async_copy(source, target, in_sem.at[i])
        for i, (source, target) in enumerate(
            (
                (feat_h, feat), (send_h, send_s), (send_h, send_v), (cw_h, cw), (cot_h, cot), (dw_h, dw),
                (src_h, src_s), (src_h, src_p),
            )
        )
    ]
    for load in loads:
        load.start()
    loads[0].wait()

    low8, row8 = lows(8), row_iota(8)
    for b in range(4):
        for x in range(8):
            v = feat[b, x].astype(F32)
            for q in range(4):
                flat[q * 256 + b * 64 + x * 8 : q * 256 + b * 64 + x * 8 + 8, :] = v[:, 128 * q : 128 * q + 128]

    def rows(q, b, y):
        return flat[pl.ds(q * 256 + b * 64 + y, 8, stride=8), :]

    def face(number, tiles):
        value = to_face(tiles).astype(BF16)
        faces[number] = value
        table[number] = value

    for b in range(4):
        for s, x in ((0, 0), (1, 7)):
            v = feat[b, x].astype(F32)
            face(b * 6 + s, [v[:, 128 * q : 128 * q + 128] for q in range(4)])
        for s, y in ((2, 0), (3, 7)):
            face(b * 6 + s, [rows(q, b, y) for q in range(4)])
        first = [rows(0, b, y) for y in range(8)]
        last = [rows(3, b, y) for y in range(8)]
        face(b * 6 + 4, [jnp.where(low8, first[2 * q], half(first[2 * q + 1])) for q in range(4)])
        face(b * 6 + 5, [jnp.where(low8, half(last[2 * q]), last[2 * q + 1]) for q in range(4)])
    table[DUMP] = jnp.zeros((16, 256), BF16)
    for b in range(4):
        key_s[b : b + 1] = jnp.full((1, 128), 8 * child_s[b], jnp.int32)
    loads[1].wait()

    def pack(j):
        peer = near_peer(j)
        for k in range(4):
            sbuf[j, k] = faces[jnp.maximum(send_s[k, peer], 0)]

    loop(NEAR, pack, unroll=3)
    key_s[4:8] = jnp.zeros((4, 128), jnp.int32)
    key_r[sub] = key_s[...]
    pl.semaphore_wait(barrier, NEAR + 4)

    def sub_copy(s, src, dst, sems):
        other = (sub + s) & (N_SUB - 1)
        return pltpu.make_async_remote_copy(
            src_ref=src(other), dst_ref=dst.at[sub], send_sem=sems.at[0], recv_sem=sems.at[1],
            device_id=grp * N_SUB + other, device_id_type=LOGICAL,
        )

    def grp_copy(s, src, dst, sems):
        other = (grp + s) & (N_GRP - 1)
        return pltpu.make_async_remote_copy(
            src_ref=src(other), dst_ref=dst(grp), send_sem=sems.at[0], recv_sem=sems.at[1],
            device_id=other * N_SUB + sub, device_id_type=LOGICAL,
        )

    def near_copy(j, dst, send_sem, recv_sem):
        return pltpu.make_async_remote_copy(
            src_ref=sbuf.at[j], dst_ref=dst, send_sem=send_sem, recv_sem=recv_sem,
            device_id=near_peer(j), device_id_type=LOGICAL,
        )

    def all_of(ref, sems):
        return pltpu.make_async_remote_copy(
            src_ref=ref, dst_ref=ref, send_sem=sems.at[0], recv_sem=sems.at[1],
            device_id=(me + 1) & (PEERS - 1), device_id_type=LOGICAL,
        )

    def key_copy(s):
        return sub_copy(s, lambda other: key_s, key_r, key_sem)

    def tg_copy(s):
        return sub_copy(s, lambda other: tg_s.at[other], tg_r, tg_sem)

    def tile_copy(s):
        return sub_copy(s, lambda other: tile_s, tile_r, tile_sem)

    def face_copy(j):
        return near_copy(j, table.at[pl.ds(LOCAL + 4 * twin(j), 4)], face_sem.at[0], face_sem.at[1])

    def back_copy(j):
        return near_copy(j, returned.at[twin(j)], face_sem.at[2], back_rs.at[twin(j)])

    def back_arrival(j):
        return near_copy(j, returned.at[j], face_sem.at[2], back_rs.at[j])

    def one_copy(s):
        return grp_copy(
            s, lambda other: convt.at[other, pl.ds(0, 112)], lambda slot: rs1.at[slot, pl.ds(0, 112)], one_sem
        )

    def oneb_copy(s):
        return grp_copy(
            s, lambda other: convt.at[other, pl.ds(112, 16)], lambda slot: rs1.at[slot, pl.ds(112, 16)], one_sem
        )

    def two_copy(s):
        return sub_copy(s, lambda other: tot.at[pl.ds(8 * other, 8)], rs2, two_sem)

    def three_copy(s):
        return sub_copy(s, lambda other: fin, ag1, three_sem)

    def four_copy(s):
        return grp_copy(s, lambda other: ag1b, lambda slot: ag2.at[slot], four_sem)

    sub_all, grp_all = pl.ds(0, N_SUB - 1), pl.ds(0, N_GRP - 1)
    key_all = all_of(key_r.at[sub_all], key_sem)
    tg_all = all_of(tg_r.at[sub_all], tg_sem)
    tile_all = all_of(tile_r.at[sub_all], tile_sem)
    face_all = all_of(table.at[pl.ds(LOCAL, SLOTS)], face_sem)
    one_all = all_of(rs1.at[grp_all], one_sem)
    two_all = all_of(rs2.at[sub_all], two_sem)
    three_all = all_of(ag1.at[sub_all], three_sem)
    four_all = all_of(ag2.at[grp_all], four_sem)

    loop(N_SUB, lambda s: key_copy(s).start(), 1)
    loop(FIRST_FACES, lambda j: face_copy(j).start())

    for load in loads[2:]:
        load.wait()
    band[...] = jnp.zeros_like(band)
    bandt[...] = jnp.zeros_like(bandt)
    for n in range(9):
        for s in range(3):
            w = cw[3 * n + s]
            band[n, 64 * s : 64 * s + 64, 0:64] = w
            band[n, 64 * s + 64 : 64 * s + 128, 64:128] = w
            d = 2 - s
            bandt[n, 0:64, 64 * d : 64 * d + 64] = w
            bandt[n, 64:128, 64 * d + 64 : 64 * d + 128] = w
    pg[...] = jnp.zeros_like(pg)
    term[TERMS] = jnp.zeros((8, 512), F32)
    chain[SLOTS] = jnp.zeros((8, 512), F32)
    dwp[0:64] = dw[...]
    dwp[64:128] = dw[...]
    coarse_grad = lax.dot_general(
        cot[0], dwp[...], (((1,), (1,)), ((), ())), preferred_element_type=F32
    ).astype(BF16)

    def voxel_key(shape, dim):
        v = lax.broadcasted_iota(jnp.int32, shape, dim)
        x, y, z = v >> 6, (v >> 3) & 7, v & 7
        spot = 16 * (x >> 1) + 4 * (y >> 1) + (z >> 1)
        inside = 4 * (x & 1) + 2 * (y & 1) + (z & 1)
        return (64 * sub + spot) * 8 + inside

    key_all.wait_recv()
    ijk = row_iota(8)
    keys = jnp.concatenate(
        [jnp.broadcast_to(key_r[s, b : b + 1, :], (8, 128)) + ijk for s in range(N_SUB) for b in range(4)], axis=0
    )
    wanted = jnp.broadcast_to(voxel_key((1, 512), 1), (512, 512))
    take = jnp.where(jnp.concatenate([keys] * 4, axis=1) == wanted, 1.0, 0.0).astype(BF16)
    tiles = jnp.dot(take, coarse_grad, preferred_element_type=F32).astype(BF16)
    tg_s[...] = tiles.reshape(N_SUB, 32, 128)
    tg_r[sub] = tg_s[sub]
    loop(N_SUB, lambda s: tg_copy(s).start(), 1)
    loop(NEAR, lambda j: face_copy(j).start(), FIRST_FACES)
    key_row = jnp.concatenate([keys[128 * q : 128 * q + 128].T for q in range(4)], axis=1)[0:1]
    place[...] = jnp.where(
        jnp.broadcast_to(key_row, (512, 512)) == jnp.broadcast_to(voxel_key((512, 1), 0), (512, 512)), 1.0, 0.0
    ).astype(BF16)
    src_v[...] = jnp.full((8, 128), -1, jnp.int32)
    src_v[0:4, 0:26] = src_p[...]
    index_tables(src_v, send_v, ids, me)
    to_scalars = pltpu.make_async_copy(ids, ids_s, in_sem.at[8])
    to_scalars.start()
    to_scalars.wait()
    face_all.wait_recv()

    def slab(b, offset):
        code = src_s[b, NUMBER[offset]]
        remote = code - LOCAL
        spot = LOCAL + 4 * near_of(((remote >> 2) - me) & (PEERS - 1)) + (remote & 3)
        return from_face(table[jnp.where(code < 0, DUMP, jnp.where(code < LOCAL, code, spot))])

    for b in range(4):
        below, above = slab(b, (0, 0, -1)), slab(b, (0, 0, 1))
        for y in range(8):
            q = y // 2
            if y % 2 == 0:
                value = jnp.where(low8, above[q], half(below[q]))
            else:
                value = jnp.where(low8, half(above[q]), below[q])
            zrim[pl.ds(b * 8 + y, 8, stride=32), :] = value
        for dy, row in ((-1, 7), (1, 0)):
            wide = widen(slab(b, (0, dy, 0)), slab(b, (0, dy, -1))[3], slab(b, (0, dy, 1))[0])
            for m in range(5):
                yrim[pl.ds(m * 256 + b * 8 + row, 8, stride=32), :] = wide[m]

    def put(m, first, value, before, after):
        count = value.shape[0]
        lanes = slice(128 * m, 128 * m + 128)
        row = row_iota(count) & 7
        pad[1, first : first + count, lanes] = value.astype(BF16)
        pad[0, first : first + count, lanes] = roll8(jnp.where(row == 7, before, value), 1).astype(BF16)
        pad[2, first : first + count, lanes] = roll8(jnp.where(row == 0, after, value), -1).astype(BF16)

    for dx, plane in ((-1, 0), (1, 9)):
        parts = [[], [], []]
        for b in range(4):
            for i, dy in enumerate((-1, 0, 1)):
                parts[i].append(
                    widen(slab(b, (dx, dy, 0)), slab(b, (dx, dy, -1))[3], slab(b, (dx, dy, 1))[0])
                )
        for m in range(5):
            before, value, after = [
                jnp.concatenate([part[b][m] for b in range(4)], axis=0) for part in parts
            ]
            put(m, plane * 32, value, before, after)
    for x in range(8):
        inside = []
        for q in range(4):
            inside.append(
                jnp.concatenate([feat[b, x][:, 128 * q : 128 * q + 128].astype(F32) for b in range(4)], axis=0)
            )
        rim = zrim[32 * x : 32 * x + 32, :]
        wide = widen(inside, rim, rim)
        for m in range(5):
            edge = yrim[m * 256 + 32 * x : m * 256 + 32 * x + 32, :]
            put(m, 32 * x + 32, wide[m], edge, edge)

    for m in range(4):
        total = None
        for n in range(9):
            sx, sy = n // 3, n % 3
            product = jnp.dot(
                pad[sy, 32 * sx : 32 * sx + 256, 128 * m : 128 * m + 256], band[n], preferred_element_type=F32
            )
            total = product if total is None else total + product
        pre[256 * m : 256 * m + 256] = total

    tg_all.wait_recv()
    grad_tile = tg_r[0].astype(F32)
    for s in range(1, N_SUB):
        grad_tile += tg_r[s].astype(F32)
    grad_tile = grad_tile.reshape(4, 8, 128)
    sub_row = lax.broadcasted_iota(jnp.int32, (4, 8, 128), 1)
    pooled = jnp.zeros((4, 8, 128), F32)
    for top in range(2):
        for deep in range(2):
            spread = jnp.where(
                sub_row < 4,
                jnp.broadcast_to(grad_tile[:, 4 * top + deep : 4 * top + deep + 1, :], (4, 8, 128)),
                jnp.broadcast_to(grad_tile[:, 4 * top + 2 + deep : 4 * top + 3 + deep, :], (4, 8, 128)),
            ).reshape(32, 128) * (1.0 / 64.0)
            total = jnp.zeros((32, 128), F32)
            for m in (2 * deep, 2 * deep + 1):
                for x in range(4 * top, 4 * top + 4):
                    u = pre[256 * m + 32 * x : 256 * m + 32 * x + 32, :]
                    g = 1.0 / (1.0 + jnp.exp(-u))
                    total += u * g
                    slope = g * (1.0 + u * (1.0 - g))
                    pg[64 + 32 * x : 96 + 32 * x, 128 * m + 128 : 128 * m + 256] = (spread * slope).astype(BF16)
            total = total + half(total)
            grouped = total.reshape(4, 8, 128)
            grouped = grouped + pltpu.roll(grouped, 7, axis=1)
            grouped = grouped + pltpu.roll(grouped, 6, axis=1)
            for mid in range(2):
                pooled = jnp.where(
                    sub_row == 4 * top + 2 * mid + deep,
                    jnp.broadcast_to(grouped[:, 4 * mid : 4 * mid + 1, :], (4, 8, 128)),
                    pooled,
                )
    pooled = pooled.reshape(32, 128) * (1.0 / 64.0)
    tile_s[...] = jnp.where(lows(32), pooled, 0.0).astype(BF16)
    tile_r[sub] = tile_s[...]
    loop(N_SUB, lambda s: tile_copy(s).start(), 1)

    for m in range(4):
        pgt[:, 256 * m : 256 * m + 256] = (
            pg[64:320, 128 * m + 128 : 128 * m + 256].astype(F32).T.astype(BF16)
        )
    low64 = lows(64)

    def keep(chunk, value):
        for g in range(N_GRP):
            convt[g, 8 * chunk : 8 * chunk + 8] = value[8 * g : 8 * g + 8]

    held = None
    for n in range(9):
        sx, sy = n // 3, n % 3
        total = None
        for m in range(4):
            product = jnp.dot(
                pgt[:, 256 * m : 256 * m + 256],
                pad[sy, 32 * sx : 32 * sx + 256, 128 * m : 128 * m + 256],
                preferred_element_type=F32,
            )
            total = product if total is None else total + product
        r0, r1 = half(total[64:128, 0:128]), half(total[64:128, 128:256])
        first = total[0:64, 0:128] + jnp.where(low64, r0, r1)
        second = total[0:64, 128:256] + r1
        at = 3 * (n // 2)
        if n % 2 == 0:
            keep(at, first)
            held = second
        else:
            turned = half(first)
            keep(at + 1, jnp.where(low64, held, turned))
            keep(at + 2, jnp.where(low64, turned, half(second)))
    keep(13, jnp.where(low64, held, 0.0))
    loop(N_GRP, lambda s: one_copy(s).start(), 1)

    for sy in range(3):
        for m in range(5):
            total = None
            for sx in range(3):
                product = lax.dot_general(
                    pg[32 * (2 - sx) : 32 * (2 - sx) + 320, 128 * m : 128 * m + 256],
                    bandt[3 * sx + sy],
                    (((1,), (1,)), ((), ())),
                    preferred_element_type=F32,
                )
                total = product if total is None else total + product
            acc_a[(sy * 5 + m) * 320 : (sy * 5 + m) * 320 + 320, :] = total

    def part(sy, m, first, count):
        return acc_a[(sy * 5 + m) * 320 + first : (sy * 5 + m) * 320 + first + count, :]

    def middle(m, first, count):
        row = row_iota(count) & 7
        return (
            part(1, m, first, count)
            + jnp.where(row < 7, roll8(part(0, m, first, count), -1), 0.0)
            + jnp.where(row > 0, roll8(part(2, m, first, count), 1), 0.0)
        )

    for x in range(8):
        wide = [middle(m, 32 * x + 32, 32) for m in range(5)]
        for q, tile in enumerate(narrow(wide)):
            inner[256 * q + 32 * x : 256 * q + 32 * x + 32, :] = tile
        zrim[32 * x : 32 * x + 32, :] = jnp.where(lows(32), wide[0], wide[4])

    planes = {}
    for dx, plane in ((-1, 0), (1, 9)):
        for b in range(4):
            first = 32 * plane + 8 * b
            planes[dx, 0, b] = [middle(m, first, 8) for m in range(5)]
            planes[dx, -1, b] = [
                jnp.where(row8 == 7, roll8(part(0, m, first, 8), -1), 0.0) for m in range(5)
            ]
            planes[dx, 1, b] = [
                jnp.where(row8 == 0, roll8(part(2, m, first, 8), 1), 0.0) for m in range(5)
            ]

    def rim(b, offset):
        dx, dy, dz = offset
        if dx == 0 and dy == 0:
            rims = [zrim[pl.ds(b * 8 + y, 8, stride=32), :] for y in range(8)]
            if dz < 0:
                return [jnp.where(low8, rims[2 * q], half(rims[2 * q + 1])) for q in range(4)]
            return [jnp.where(low8, half(rims[2 * q]), rims[2 * q + 1]) for q in range(4)]
        if dx != 0:
            wide = planes[dx, dy, b]
        else:
            sy, row = (0, 0) if dy < 0 else (2, 7)
            wide = [
                acc_a[pl.ds((sy * 5 + m) * 320 + 32 + b * 8 + row, 8, stride=32), :] for m in range(5)
            ]
        if dz == 0:
            return narrow(wide)
        if dz > 0:
            return [jnp.where(low8, half(wide[4]), 0.0), None, None, None]
        return [None, None, None, jnp.where(low8, 0.0, half(wide[0]))]

    for b in range(4):
        for t, offset in enumerate(OFFSETS):
            earlier = ids_s[b, t]
            for q, tile in enumerate(rim(b, offset)):
                value = term[earlier, :, 128 * q : 128 * q + 128]
                term[26 * b + t, :, 128 * q : 128 * q + 128] = value if tile is None else value + tile

    face_all.wait_send()

    def leave(j):
        for k in range(4):
            value = term[ids_s[4 + k, j]]
            sbuf[j, k] = to_face([value[:, 128 * q : 128 * q + 128] for q in range(4)]).astype(BF16)
        back_copy(j).start()

    loop(11, leave)

    tile_all.wait_recv()
    coarse_in = jnp.dot(place[...], tile_r[...].reshape(512, 128), preferred_element_type=F32)
    dwp[64:128] = jnp.zeros((64, 128), BF16)
    down = jnp.dot(coarse_in.T.astype(BF16), cot[0], preferred_element_type=F32)
    for g in range(N_GRP):
        convt[g, 112:120] = down[8 * g : 8 * g + 8]
        convt[g, 120:128] = jnp.zeros((8, 128), F32)
    loop(N_GRP, lambda s: oneb_copy(s).start(), 1)
    coarse[0] = jnp.dot(coarse_in.astype(BF16), dwp[...], preferred_element_type=F32).astype(BF16)
    coarse_store = pltpu.make_async_copy(coarse, coarse_h, out_sem.at[0])
    coarse_store.start()
    rs1[grp] = convt[grp]

    one_all.wait_recv()
    total = rs1[0]
    for g in range(1, N_GRP):
        total += rs1[g]
    tot[...] = total
    loop(N_SUB, lambda s: two_copy(s).start(), 1)
    loop(22, leave, 11)
    rs2[sub] = tot[pl.ds(pl.multiple_of(8 * sub, 8), 8), :]
    two_all.wait_recv()
    total = rs2[0]
    for s in range(1, N_SUB):
        total += rs2[s]
    fin[...] = total
    loop(N_SUB, lambda s: three_copy(s).start(), 1)
    loop(NEAR, leave, 22)
    ag1[sub] = fin[...]
    three_all.wait_recv()
    ag1b[...] = ag1[...].reshape(128, 128).astype(BF16)
    loop(N_GRP, lambda s: four_copy(s).start(), 1)
    own_sums = pltpu.make_async_copy(ag1b, ag2.at[grp], out_sem.at[2])
    own_sums.start()

    def take_back(j):
        back_arrival(j).wait_recv()
        peer = near_peer(j)
        for k in range(4):
            value = chain[ids_s[9 + k, peer]]
            tiles = from_face(returned[j, k])
            for q in range(4):
                chain[4 * j + k, :, 128 * q : 128 * q + 128] = value[:, 128 * q : 128 * q + 128] + tiles[q]

    loop(NEAR, take_back, unroll=3)

    face_sums = [term[ids_s[8, f]] + chain[ids_s[13, f]] for f in range(LOCAL)]

    def tile_of(f, q):
        return face_sums[f][:, 128 * q : 128 * q + 128]

    for b in range(4):
        for f, row in ((2, 0), (3, 7)):
            for q in range(4):
                yrim[pl.ds(q * 256 + b * 8 + row, 8, stride=32), :] = tile_of(6 * b + f, q)
        for y in range(8):
            below, above = tile_of(6 * b + 4, y // 2), tile_of(6 * b + 5, y // 2)
            if y % 2 == 0:
                value = jnp.where(low8, below, half(above))
            else:
                value = jnp.where(low8, half(below), above)
            zrim[pl.ds(b * 8 + y, 8, stride=32), :] = value
    edge = jnp.logical_or(row8 == 0, row8 == 7)
    for b in range(4):
        for x in range(8):
            at = 32 * x + 8 * b
            rim_z = zrim[at : at + 8, :]
            tiles = []
            for q in range(4):
                value = inner[256 * q + at : 256 * q + at + 8, :]
                if x == 0 or x == 7:
                    value = value + tile_of(6 * b + (0 if x == 0 else 1), q)
                value = value + jnp.where(edge, yrim[256 * q + at : 256 * q + at + 8, :], 0.0)
                if q == 0:
                    value = value + jnp.where(low8, rim_z, 0.0)
                if q == 3:
                    value = value + jnp.where(low8, 0.0, rim_z)
                tiles.append(value)
            grad[b, x] = jnp.concatenate(tiles, axis=1).astype(BF16)
    grad_store = pltpu.make_async_copy(grad, grad_h, out_sem.at[1])
    grad_store.start()

    own_sums.wait()
    four_all.wait_recv()

    for group in (key_all, tg_all, tile_all, one_all, two_all, three_all, four_all):
        group.wait_send()
    pltpu.make_async_remote_copy(
        src_ref=sbuf, dst_ref=returned, send_sem=face_sem.at[2], recv_sem=face_sem.at[1],
        device_id=(me + 1) & (PEERS - 1), device_id_type=LOGICAL,
    ).wait_send()
    for store in (coarse_store, grad_store):
        store.wait()


def finish_kernel(
    coarse, grad, sums, coarse_o, grad_o, conv_o, down_o, coarse_v, grad_v, ag2, conv_v, down_v, loaded, sems
):
    loads = [
        pltpu.make_async_copy(source, target, loaded.at[i])
        for i, (source, target) in enumerate(((sums, ag2), (coarse, coarse_v), (grad, grad_v)))
    ]
    for load in loads:
        load.start()
    for load in loads:
        load.wait()
    stores = [
        pltpu.make_async_copy(coarse_v, coarse_o, sems.at[0]), pltpu.make_async_copy(grad_v, grad_o, sems.at[1])
    ]
    for store in stores:
        store.start()
    got = [ag2[g].astype(F32) for g in range(N_GRP)]

    def save(source, target, number):
        stores.append(pltpu.make_async_copy(source, target, sems.at[number]))
        stores[-1].start()

    for s in range(15):
        value = jnp.concatenate([got[g][8 * s : 8 * s + 8] for g in range(N_GRP)], axis=0)
        if s == 14:
            down_v[...] = value
            save(down_v, down_o, 6)
            continue
        turned = value.T
        conv_v[2 * s] = turned[0:64]
        if s < 13:
            conv_v[2 * s + 1] = turned[64:128]
        if s in (3, 6, 9, 13):
            first, last = {3: (0, 8), 6: (8, 14), 9: (14, 20), 13: (20, 27)}[s]
            part = pl.ds(first, last - first)
            save(conv_v.at[part], conv_o.at[part], {3: 2, 6: 3, 9: 4, 13: 5}[s])
    for store in stores:
        store.wait()


def dma(*shape):
    return pltpu.SemaphoreType.DMA(shape)


def per_device(features, conv_weight, down_weight, cotangent, src_table, send_list, child_map):
    hbm = pl.BlockSpec(memory_space=pl.ANY)
    vmem, smem, i32 = pltpu.VMEM, pltpu.SMEM, jnp.int32
    coarse, grad_input, sums = pl.pallas_call(
        block_kernel,
        out_shape=(
            jax.ShapeDtypeStruct((1, 512, 128), BF16),
            jax.ShapeDtypeStruct((4, 8, 8, 512), BF16),
            jax.ShapeDtypeStruct((N_GRP, 128, 128), BF16),
        ),
        in_specs=[hbm] * 6 + [pl.BlockSpec(memory_space=pltpu.SMEM)],
        out_specs=(hbm,) * 3,
        scratch_shapes=[
            vmem((4, 8, 8, 512), BF16), vmem((27, C, C), BF16), vmem((C, 128), BF16), vmem((1, 512, 128), BF16),
            smem((4, 26), i32), vmem((4, 26), i32), vmem((8, 128), i32),
            smem((4, PEERS), i32), vmem((4, PEERS), i32), vmem((16, 128), i32), smem((16, 128), i32),
            vmem((1024, 128), F32),
            vmem((LOCAL, 16, 256), BF16),
            vmem((TABLE, 16, 256), BF16),
            vmem((NEAR, 4, 16, 256), BF16),
            vmem((NEAR, 4, 16, 256), BF16),
            vmem((8, 128), i32), vmem((N_SUB, 8, 128), i32),
            vmem((128, 128), BF16),
            vmem((N_SUB, 32, 128), BF16), vmem((N_SUB, 32, 128), BF16),
            vmem((512, 512), BF16),
            vmem((9, 256, 128), BF16), vmem((9, 128, 256), BF16),
            vmem((256, 128), F32), vmem((1280, 128), F32),
            vmem((3, 320, 640), BF16),
            vmem((1024, 128), F32),
            vmem((384, 768), BF16),
            vmem((128, 1024), BF16),
            vmem((15 * 320, 128), F32),
            vmem((TERMS + 1, 8, 512), F32),
            vmem((1024, 128), F32),
            vmem((32, 128), BF16), vmem((N_SUB, 32, 128), BF16),
            vmem((N_GRP, 128, 128), F32), vmem((N_GRP, 128, 128), F32), vmem((128, 128), F32),
            vmem((N_SUB, 8, 128), F32), vmem((8, 128), F32), vmem((N_SUB, 8, 128), F32),
            vmem((128, 128), BF16),
            vmem((SLOTS + 1, 8, 512), F32),
            vmem((1, 512, 128), BF16), vmem((4, 8, 8, 512), BF16),
        ]
        + [dma(3), dma(NEAR)]
        + [dma(2)] * 7
        + [dma(9), dma(3)],
        compiler_params=pltpu.CompilerParams(
            collective_id=0, has_side_effects=True, vmem_limit_bytes=VMEM_LIMIT
        ),
        name="block",
    )(features, conv_weight, down_weight, cotangent, src_table, send_list[0].T, child_map)
    return pl.pallas_call(
        finish_kernel,
        out_shape=(
            jax.ShapeDtypeStruct((1, 512, 128), BF16),
            jax.ShapeDtypeStruct((4, 8, 8, 512), BF16),
            jax.ShapeDtypeStruct((27, C, C), F32),
            jax.ShapeDtypeStruct((C, 128), F32),
        ),
        in_specs=[hbm] * 3,
        out_specs=(hbm,) * 4,
        scratch_shapes=[
            vmem((1, 512, 128), BF16), vmem((4, 8, 8, 512), BF16),
            vmem((N_GRP, 128, 128), BF16), vmem((27, C, C), F32), vmem((C, 128), F32), dma(3), dma(7),
        ],
        compiler_params=pltpu.CompilerParams(vmem_limit_bytes=VMEM_LIMIT),
        name="finish",
    )(coarse, grad_input, sums)


def solution(mesh):
    both = ("grp", "sub")
    placed = (
        P(both, None, None, None),
        P(),
        P(),
        P(both, None, None),
        P(both, None),
        P(both, None, None),
        P(both),
    )
    return jax.shard_map(
        per_device,
        mesh=mesh,
        in_specs=placed,
        out_specs=(P(both, None, None), P(both, None, None, None), P(), P()),
        check_vma=False,
    )
```

```python
import jax
import jax.numpy as jnp
from jax import lax
from jax.experimental import pallas as pl
from jax.experimental.pallas import tpu as pltpu
from jax.sharding import PartitionSpec as P

LOGICAL = pl.DeviceIdType.LOGICAL
N_GRP, N_SUB = 8, 16
PEERS = N_GRP * N_SUB
NEAR = 33
C = 64
F32, BF16 = jnp.float32, jnp.bfloat16
LOCAL = 24
DUMP = LOCAL + 4 * NEAR
TABLE = DUMP + 4
VMEM_LIMIT = 58 * 1024 * 1024
TERMS = 4 * 26
FIRST_FACES = NEAR
CUTS = (8, 20)
SLOTS = 4 * NEAR

OFFSETS = [
    (x, y, z)
    for x in (-1, 0, 1)
    for y in (-1, 0, 1)
    for z in (-1, 0, 1)
    if (x, y, z) != (0, 0, 0)
]
NUMBER = {offset: number for number, offset in enumerate(OFFSETS)}


def step_of(j):
    return jnp.where(j < 16, j + 1, jnp.where(j == 16, 64, j + 95))


def twin(j):
    return NEAR - 1 - j


def near_of(step):
    return jnp.where(step <= 16, step - 1, jnp.where(step == 64, 16, step - 95))


def lane_iota(rows):
    return lax.broadcasted_iota(jnp.int32, (rows, 128), 1)


def row_iota(rows):
    return lax.broadcasted_iota(jnp.int32, (rows, 128), 0)


def half(tile):
    return pltpu.roll(tile, 64, axis=1)


def lows(rows):
    return lane_iota(rows) < 64


def to_face(tiles):
    top = jnp.concatenate([tiles[0], tiles[1]], axis=1)
    bottom = jnp.concatenate([tiles[2], tiles[3]], axis=1)
    return jnp.concatenate([top, bottom], axis=0)


def from_face(face):
    face = face.astype(F32)
    return [face[0:8, 0:128], face[0:8, 128:256], face[8:16, 0:128], face[8:16, 128:256]]


def widen(tiles, below, above):
    low = lows(tiles[0].shape[0])
    rolled = [half(tile) for tile in tiles]
    result = [jnp.where(low, half(below), rolled[0])]
    for m in range(1, 4):
        result.append(jnp.where(low, rolled[m - 1], rolled[m]))
    result.append(jnp.where(low, rolled[3], half(above)))
    return result


def narrow(tiles):
    low = lows(tiles[0].shape[0])
    rolled = [half(tile) for tile in tiles]
    return [jnp.where(low, rolled[q], rolled[q + 1]) for q in range(4)]


def roll8(value, shift):
    rows = value.shape[0]
    grouped = value.reshape(rows // 8, 8, 128)
    return pltpu.roll(grouped, shift % 8, axis=1).reshape(rows, 128)

def loop(count, body, start=0, unroll=True):
    def step(i, _):
        body(i)
        return 0

    lax.fori_loop(start, count, step, 0, unroll=unroll)


def column_max(value):
    best = value[0:8]
    for i in range(1, 16):
        best = jnp.maximum(best, value[8 * i : 8 * i + 8])
    for shift in (4, 2, 1):
        best = jnp.maximum(best, pltpu.roll(best, shift, axis=0))
    return best


def index_tables(src_v, send_v, ids, me):
    whole = (128, 128)
    below = lax.broadcasted_iota(jnp.int32, whole, 0)
    along = lax.broadcasted_iota(jnp.int32, whole, 1)
    rows = [jnp.broadcast_to(src_v[b : b + 1, :], whole) for b in range(4)]
    columns = [row.T for row in rows]

    def pick(cases, none):
        best = None
        for match, value in cases:
            value = jnp.where(match, value, -1)
            best = value if best is None else jnp.maximum(best, value)
        best = column_max(best)
        return jnp.where(best < 0, none, best)[0:1]

    for b in range(4):
        cases = []
        for c in range(b + 1):
            match = jnp.logical_and(columns[c] == rows[b], columns[c] >= 0)
            if c == b:
                match = jnp.logical_and(match, below < along)
            cases.append((match, 26 * c + below))
        ids[b : b + 1, :] = pick(cases, TERMS)
    for k in range(4):
        code = jnp.where(along < NEAR, LOCAL + 4 * ((me + step_of(along)) & (PEERS - 1)) + k, -5)
        ids[4 + k : 5 + k, :] = pick([(columns[b] == code, 26 * b + below) for b in range(4)], TERMS)
    code = jnp.where(along < LOCAL, along, -5)
    ids[8:9, :] = pick([(columns[b] == code, 26 * b + below) for b in range(4)], TERMS)

    def number(device):
        return 4 * jnp.clip(near_of((device - me) & (PEERS - 1)), 0, NEAR - 1)

    rows = [jnp.broadcast_to(send_v[k : k + 1, :], whole) for k in range(4)]
    columns = [row.T for row in rows]
    first, second = number(below), number(along)
    for k in range(4):
        cases = []
        for c in range(4):
            match = jnp.logical_and(columns[c] == rows[k], columns[c] >= 0)
            cases.append((jnp.logical_and(match, first + c < second + k), first + c))
        ids[9 + k : 10 + k, :] = pick(cases, SLOTS)
    ids[13:14, :] = pick([(columns[c] == along, first + c) for c in range(4)], SLOTS)


def block_kernel(
    feat_h, cw_h, dw_h, cot_h, src_h, send_h, child_s,
    coarse_h, grad_h, ag2,
    feat, cw, dw, cot, src_s, src_p, src_v, send_s, send_v, ids, ids_s,
    flat, faces, table, sbuf, returned, key_s, key_r, dwp, tg_s, tg_r, place,
    band, bandt, zrim, yrim, pad, pre, pg, pgt, acc_a, term, inner,
    tile_s, tile_r, convt, convb, rs1, tot, rs2, fin, ag1, ag1b, chain, coarse, grad,
    face_sem, back_rs, key_sem, tg_sem, tile_sem, one_sem, two_sem, three_sem, four_sem, in_sem, out_sem,
):
    grp, sub = lax.axis_index("grp"), lax.axis_index("sub")
    me = grp * N_SUB + sub

    barrier = pltpu.get_barrier_semaphore()

    def signal(peer):
        pl.semaphore_signal(barrier, inc=1, device_id=peer, device_id_type=LOGICAL)

    def near_peer(j):
        return (me + step_of(j)) & (PEERS - 1)

    loop(NEAR, lambda j: signal(near_peer(j)))
    for far in (2, 3, 5, 6):
        signal(((grp + far) & (N_GRP - 1)) * N_SUB + sub)

    loads = [
        pltpu.make_async_copy(source, target, in_sem.at[i])
        for i, (source, target) in enumerate(
            (
                (feat_h, feat), (send_h, send_s), (send_h, send_v), (cw_h, cw), (cot_h, cot), (dw_h, dw),
                (src_h, src_s), (src_h, src_p),
            )
        )
    ]
    for load in loads:
        load.start()
    loads[0].wait()

    low8, row8 = lows(8), row_iota(8)
    for b in range(4):
        for x in range(8):
            v = feat[b, x].astype(F32)
            for q in range(4):
                flat[q * 256 + b * 64 + x * 8 : q * 256 + b * 64 + x * 8 + 8, :] = v[:, 128 * q : 128 * q + 128]

    def rows(q, b, y):
        return flat[pl.ds(q * 256 + b * 64 + y, 8, stride=8), :]

    def face(number, tiles):
        value = to_face(tiles).astype(BF16)
        faces[number] = value
        table[number] = value

    for b in range(4):
        for s, x in ((0, 0), (1, 7)):
            v = feat[b, x].astype(F32)
            face(b * 6 + s, [v[:, 128 * q : 128 * q + 128] for q in range(4)])
        for s, y in ((2, 0), (3, 7)):
            face(b * 6 + s, [rows(q, b, y) for q in range(4)])
        first = [rows(0, b, y) for y in range(8)]
        last = [rows(3, b, y) for y in range(8)]
        face(b * 6 + 4, [jnp.where(low8, first[2 * q], half(first[2 * q + 1])) for q in range(4)])
        face(b * 6 + 5, [jnp.where(low8, half(last[2 * q]), last[2 * q + 1]) for q in range(4)])
    table[DUMP] = jnp.zeros((16, 256), BF16)
    for b in range(4):
        key_s[b : b + 1] = jnp.full((1, 128), 8 * child_s[b], jnp.int32)
    loads[1].wait()

    def pack(j):
        peer = near_peer(j)
        for k in range(4):
            sbuf[j, k] = faces[jnp.maximum(send_s[k, peer], 0)]

    loop(NEAR, pack, unroll=3)
    key_s[4:8] = jnp.zeros((4, 128), jnp.int32)
    key_r[sub] = key_s[...]
    pl.semaphore_wait(barrier, NEAR + 4)

    def sub_copy(s, src, dst, sems):
        other = (sub + s) & (N_SUB - 1)
        return pltpu.make_async_remote_copy(
            src_ref=src(other), dst_ref=dst.at[sub], send_sem=sems.at[0], recv_sem=sems.at[1],
            device_id=grp * N_SUB + other, device_id_type=LOGICAL,
        )

    def grp_copy(s, src, dst, sems):
        other = (grp + s) & (N_GRP - 1)
        return pltpu.make_async_remote_copy(
            src_ref=src(other), dst_ref=dst(grp), send_sem=sems.at[0], recv_sem=sems.at[1],
            device_id=other * N_SUB + sub, device_id_type=LOGICAL,
        )

    def near_copy(j, dst, send_sem, recv_sem):
        return pltpu.make_async_remote_copy(
            src_ref=sbuf.at[j], dst_ref=dst, send_sem=send_sem, recv_sem=recv_sem,
            device_id=near_peer(j), device_id_type=LOGICAL,
        )

    def all_of(ref, sems):
        return pltpu.make_async_remote_copy(
            src_ref=ref, dst_ref=ref, send_sem=sems.at[0], recv_sem=sems.at[1],
            device_id=(me + 1) & (PEERS - 1), device_id_type=LOGICAL,
        )

    def key_copy(s):
        return sub_copy(s, lambda other: key_s, key_r, key_sem)

    def tg_copy(s):
        return sub_copy(s, lambda other: tg_s.at[other], tg_r, tg_sem)

    def tile_copy(s):
        return sub_copy(s, lambda other: tile_s, tile_r, tile_sem)

    def face_copy(j):
        return near_copy(j, table.at[pl.ds(LOCAL + 4 * twin(j), 4)], face_sem.at[0], face_sem.at[1])

    def back_copy(j):
        return near_copy(j, returned.at[twin(j)], face_sem.at[2], back_rs.at[twin(j)])

    def back_arrival(j):
        return near_copy(j, returned.at[j], face_sem.at[2], back_rs.at[j])

    def one_copy(s):
        return grp_copy(s, lambda other: convb.at[other], lambda slot: rs1.at[slot], one_sem)

    def two_copy(s):
        return sub_copy(s, lambda other: tot.at[pl.ds(8 * other, 8)], rs2, two_sem)

    def three_copy(s):
        return sub_copy(s, lambda other: fin, ag1, three_sem)

    def four_copy(s):
        return grp_copy(s, lambda other: ag1b, lambda slot: ag2.at[slot], four_sem)

    sub_all, grp_all = pl.ds(0, N_SUB - 1), pl.ds(0, N_GRP - 1)
    key_all = all_of(key_r.at[sub_all], key_sem)
    tg_all = all_of(tg_r.at[sub_all], tg_sem)
    tile_all = all_of(tile_r.at[sub_all], tile_sem)
    face_all = all_of(table.at[pl.ds(LOCAL, SLOTS)], face_sem)
    one_all = all_of(rs1.at[grp_all], one_sem)
    two_all = all_of(rs2.at[sub_all], two_sem)
    three_all = all_of(ag1.at[sub_all], three_sem)
    four_all = all_of(ag2.at[grp_all], four_sem)

    loop(N_SUB, lambda s: key_copy(s).start(), 1)
    loop(FIRST_FACES, lambda j: face_copy(j).start())

    for load in loads[2:]:
        load.wait()
    band[...] = jnp.zeros_like(band)
    bandt[...] = jnp.zeros_like(bandt)
    for n in range(9):
        for s in range(3):
            w = cw[3 * n + s]
            band[n, 64 * s : 64 * s + 64, 0:64] = w
            band[n, 64 * s + 64 : 64 * s + 128, 64:128] = w
            d = 2 - s
            bandt[n, 0:64, 64 * d : 64 * d + 64] = w
            bandt[n, 64:128, 64 * d + 64 : 64 * d + 128] = w
    pg[...] = jnp.zeros_like(pg)
    term[TERMS] = jnp.zeros((8, 512), F32)
    chain[SLOTS] = jnp.zeros((8, 512), F32)
    dwp[0:64] = dw[...]
    dwp[64:128] = dw[...]
    def voxel_key(shape, dim):
        v = lax.broadcasted_iota(jnp.int32, shape, dim)
        x, y, z = v >> 6, (v >> 3) & 7, v & 7
        spot = 16 * (x >> 1) + 4 * (y >> 1) + (z >> 1)
        inside = 4 * (x & 1) + 2 * (y & 1) + (z & 1)
        return (64 * sub + spot) * 8 + inside

    key_all.wait_recv()
    ijk = row_iota(8)
    keys = jnp.concatenate(
        [jnp.broadcast_to(key_r[s, b : b + 1, :], (8, 128)) + ijk for s in range(N_SUB) for b in range(4)], axis=0
    )
    wanted = jnp.broadcast_to(voxel_key((1, 512), 1), (512, 512))
    take = jnp.where(jnp.concatenate([keys] * 4, axis=1) == wanted, 1.0, 0.0).astype(BF16)
    tiles = jnp.dot(take, cot[0], preferred_element_type=F32).astype(BF16)
    tg_s[...] = tiles.reshape(N_SUB, 32, 128)
    tg_r[sub] = tg_s[sub]
    loop(N_SUB, lambda s: tg_copy(s).start(), 1)
    loop(NEAR, lambda j: face_copy(j).start(), FIRST_FACES)
    key_row = jnp.concatenate([keys[128 * q : 128 * q + 128].T for q in range(4)], axis=1)[0:1]
    place[...] = jnp.where(
        jnp.broadcast_to(key_row, (512, 512)) == jnp.broadcast_to(voxel_key((512, 1), 0), (512, 512)), 1.0, 0.0
    ).astype(BF16)
    src_v[...] = jnp.full((8, 128), -1, jnp.int32)
    src_v[0:4, 0:26] = src_p[...]
    index_tables(src_v, send_v, ids, me)
    to_scalars = pltpu.make_async_copy(ids, ids_s, in_sem.at[8])
    to_scalars.start()
    to_scalars.wait()
    face_all.wait_recv()

    def slab(b, offset):
        code = src_s[b, NUMBER[offset]]
        remote = code - LOCAL
        spot = LOCAL + 4 * near_of(((remote >> 2) - me) & (PEERS - 1)) + (remote & 3)
        return from_face(table[jnp.where(code < 0, DUMP, jnp.where(code < LOCAL, code, spot))])

    for b in range(4):
        below, above = slab(b, (0, 0, -1)), slab(b, (0, 0, 1))
        for y in range(8):
            q = y // 2
            if y % 2 == 0:
                value = jnp.where(low8, above[q], half(below[q]))
            else:
                value = jnp.where(low8, half(above[q]), below[q])
            zrim[pl.ds(b * 8 + y, 8, stride=32), :] = value
        for dy, row in ((-1, 7), (1, 0)):
            wide = widen(slab(b, (0, dy, 0)), slab(b, (0, dy, -1))[3], slab(b, (0, dy, 1))[0])
            for m in range(5):
                yrim[pl.ds(m * 256 + b * 8 + row, 8, stride=32), :] = wide[m]

    def put(m, first, value, before, after):
        count = value.shape[0]
        lanes = slice(128 * m, 128 * m + 128)
        row = row_iota(count) & 7
        pad[1, first : first + count, lanes] = value.astype(BF16)
        pad[0, first : first + count, lanes] = roll8(jnp.where(row == 7, before, value), 1).astype(BF16)
        pad[2, first : first + count, lanes] = roll8(jnp.where(row == 0, after, value), -1).astype(BF16)

    for dx, plane in ((-1, 0), (1, 9)):
        parts = [[], [], []]
        for b in range(4):
            for i, dy in enumerate((-1, 0, 1)):
                parts[i].append(
                    widen(slab(b, (dx, dy, 0)), slab(b, (dx, dy, -1))[3], slab(b, (dx, dy, 1))[0])
                )
        for m in range(5):
            before, value, after = [
                jnp.concatenate([part[b][m] for b in range(4)], axis=0) for part in parts
            ]
            put(m, plane * 32, value, before, after)
    for x in range(8):
        inside = []
        for q in range(4):
            inside.append(
                jnp.concatenate([feat[b, x][:, 128 * q : 128 * q + 128].astype(F32) for b in range(4)], axis=0)
            )
        rim = zrim[32 * x : 32 * x + 32, :]
        wide = widen(inside, rim, rim)
        for m in range(5):
            edge = yrim[m * 256 + 32 * x : m * 256 + 32 * x + 32, :]
            put(m, 32 * x + 32, wide[m], edge, edge)

    for m in range(4):
        total = None
        for n in range(9):
            sx, sy = n // 3, n % 3
            product = jnp.dot(
                pad[sy, 32 * sx : 32 * sx + 256, 128 * m : 128 * m + 256], band[n], preferred_element_type=F32
            )
            total = product if total is None else total + product
        pre[256 * m : 256 * m + 256] = total

    tg_all.wait_recv()
    grad_tile = tg_r[0].astype(F32)
    for s in range(1, N_SUB):
        grad_tile += tg_r[s].astype(F32)
    cot_rows = grad_tile.astype(BF16)
    grad_tile = (
        lax.dot_general(cot_rows, dwp[...], (((1,), (1,)), ((), ())), preferred_element_type=F32)
        .astype(BF16)
        .astype(F32)
        .reshape(4, 8, 128)
    )
    sub_row = lax.broadcasted_iota(jnp.int32, (4, 8, 128), 1)
    pooled = jnp.zeros((4, 8, 128), F32)
    for top in range(2):
        for deep in range(2):
            spread = jnp.where(
                sub_row < 4,
                jnp.broadcast_to(grad_tile[:, 4 * top + deep : 4 * top + deep + 1, :], (4, 8, 128)),
                jnp.broadcast_to(grad_tile[:, 4 * top + 2 + deep : 4 * top + 3 + deep, :], (4, 8, 128)),
            ).reshape(32, 128) * (1.0 / 64.0)
            total = jnp.zeros((32, 128), F32)
            for m in (2 * deep, 2 * deep + 1):
                for x in range(4 * top, 4 * top + 4):
                    u = pre[256 * m + 32 * x : 256 * m + 32 * x + 32, :]
                    g = 1.0 / (1.0 + jnp.exp(-u))
                    total += u * g
                    slope = g * (1.0 + u * (1.0 - g))
                    pg[64 + 32 * x : 96 + 32 * x, 128 * m + 128 : 128 * m + 256] = (spread * slope).astype(BF16)
            total = total + half(total)
            grouped = total.reshape(4, 8, 128)
            grouped = grouped + pltpu.roll(grouped, 7, axis=1)
            grouped = grouped + pltpu.roll(grouped, 6, axis=1)
            for mid in range(2):
                pooled = jnp.where(
                    sub_row == 4 * top + 2 * mid + deep,
                    jnp.broadcast_to(grouped[:, 4 * mid : 4 * mid + 1, :], (4, 8, 128)),
                    pooled,
                )
    pooled = pooled.reshape(32, 128) * (1.0 / 64.0)
    pooled = jnp.where(lows(32), pooled, 0.0)
    tile_s[...] = pooled.astype(BF16)
    down = jnp.dot(pooled.T.astype(BF16), cot_rows, preferred_element_type=F32)
    for g in range(N_GRP):
        convt[g, 112:120] = down[8 * g : 8 * g + 8]
        convt[g, 120:128] = jnp.zeros((8, 128), F32)
    tile_r[sub] = tile_s[...]
    loop(N_SUB, lambda s: tile_copy(s).start(), 1)

    for m in range(4):
        pgt[:, 256 * m : 256 * m + 256] = (
            pg[64:320, 128 * m + 128 : 128 * m + 256].astype(F32).T.astype(BF16)
        )
    low64 = lows(64)

    def keep(chunk, value):
        for g in range(N_GRP):
            convt[g, 8 * chunk : 8 * chunk + 8] = value[8 * g : 8 * g + 8]

    held = None
    for n in range(9):
        sx, sy = n // 3, n % 3
        total = None
        for m in range(4):
            product = jnp.dot(
                pgt[:, 256 * m : 256 * m + 256],
                pad[sy, 32 * sx : 32 * sx + 256, 128 * m : 128 * m + 256],
                preferred_element_type=F32,
            )
            total = product if total is None else total + product
        r0, r1 = half(total[64:128, 0:128]), half(total[64:128, 128:256])
        first = total[0:64, 0:128] + jnp.where(low64, r0, r1)
        second = total[0:64, 128:256] + r1
        at = 3 * (n // 2)
        if n % 2 == 0:
            keep(at, first)
            held = second
        else:
            turned = half(first)
            keep(at + 1, jnp.where(low64, held, turned))
            keep(at + 2, jnp.where(low64, turned, half(second)))
    keep(13, jnp.where(low64, held, 0.0))
    convb[...] = convt[...].astype(BF16)
    rs1[grp] = jnp.zeros((128, 128), BF16)
    loop(N_GRP, lambda s: one_copy(s).start(), 1)

    for sy in range(3):
        for m in range(5):
            total = None
            for sx in range(3):
                product = lax.dot_general(
                    pg[32 * (2 - sx) : 32 * (2 - sx) + 320, 128 * m : 128 * m + 256],
                    bandt[3 * sx + sy],
                    (((1,), (1,)), ((), ())),
                    preferred_element_type=F32,
                )
                total = product if total is None else total + product
            acc_a[(sy * 5 + m) * 320 : (sy * 5 + m) * 320 + 320, :] = total

    def part(sy, m, first, count):
        return acc_a[(sy * 5 + m) * 320 + first : (sy * 5 + m) * 320 + first + count, :]

    def middle(m, first, count):
        row = row_iota(count) & 7
        return (
            part(1, m, first, count)
            + jnp.where(row < 7, roll8(part(0, m, first, count), -1), 0.0)
            + jnp.where(row > 0, roll8(part(2, m, first, count), 1), 0.0)
        )

    for x in range(8):
        wide = [middle(m, 32 * x + 32, 32) for m in range(5)]
        for q, tile in enumerate(narrow(wide)):
            inner[256 * q + 32 * x : 256 * q + 32 * x + 32, :] = tile
        zrim[32 * x : 32 * x + 32, :] = jnp.where(lows(32), wide[0], wide[4])

    planes = {}
    for dx, plane in ((-1, 0), (1, 9)):
        for b in range(4):
            first = 32 * plane + 8 * b
            planes[dx, 0, b] = [middle(m, first, 8) for m in range(5)]
            planes[dx, -1, b] = [
                jnp.where(row8 == 7, roll8(part(0, m, first, 8), -1), 0.0) for m in range(5)
            ]
            planes[dx, 1, b] = [
                jnp.where(row8 == 0, roll8(part(2, m, first, 8), 1), 0.0) for m in range(5)
            ]

    def rim(b, offset):
        dx, dy, dz = offset
        if dx == 0 and dy == 0:
            rims = [zrim[pl.ds(b * 8 + y, 8, stride=32), :] for y in range(8)]
            if dz < 0:
                return [jnp.where(low8, rims[2 * q], half(rims[2 * q + 1])) for q in range(4)]
            return [jnp.where(low8, half(rims[2 * q]), rims[2 * q + 1]) for q in range(4)]
        if dx != 0:
            wide = planes[dx, dy, b]
        else:
            sy, row = (0, 0) if dy < 0 else (2, 7)
            wide = [
                acc_a[pl.ds((sy * 5 + m) * 320 + 32 + b * 8 + row, 8, stride=32), :] for m in range(5)
            ]
        if dz == 0:
            return narrow(wide)
        if dz > 0:
            return [jnp.where(low8, half(wide[4]), 0.0), None, None, None]
        return [None, None, None, jnp.where(low8, 0.0, half(wide[0]))]

    for b in range(4):
        for t, offset in enumerate(OFFSETS):
            earlier = ids_s[b, t]
            for q, tile in enumerate(rim(b, offset)):
                value = term[earlier, :, 128 * q : 128 * q + 128]
                term[26 * b + t, :, 128 * q : 128 * q + 128] = value if tile is None else value + tile

    face_all.wait_send()

    def leave(j):
        for k in range(4):
            value = term[ids_s[4 + k, j]]
            sbuf[j, k] = to_face([value[:, 128 * q : 128 * q + 128] for q in range(4)]).astype(BF16)
        back_copy(j).start()

    loop(CUTS[0], leave)

    one_all.wait_recv()
    total = convt[grp]
    for g in range(N_GRP):
        total += rs1[g].astype(F32)
    tot[...] = total
    loop(N_SUB, lambda s: two_copy(s).start(), 1)
    loop(CUTS[1], leave, CUTS[0])
    rs2[sub] = tot[pl.ds(pl.multiple_of(8 * sub, 8), 8), :]
    two_all.wait_recv()
    total = rs2[0]
    for s in range(1, N_SUB):
        total += rs2[s]
    fin[...] = total
    loop(N_SUB, lambda s: three_copy(s).start(), 1)
    loop(NEAR, leave, CUTS[1])

    tile_all.wait_recv()
    coarse_in = jnp.dot(place[...], tile_r[...].reshape(512, 128), preferred_element_type=F32)
    dwp[64:128] = jnp.zeros((64, 128), BF16)
    coarse[0] = jnp.dot(coarse_in.astype(BF16), dwp[...], preferred_element_type=F32).astype(BF16)
    coarse_store = pltpu.make_async_copy(coarse, coarse_h, out_sem.at[0])
    coarse_store.start()
    ag1[sub] = fin[...]
    three_all.wait_recv()
    ag1b[...] = ag1[...].reshape(128, 128).astype(BF16)
    loop(N_GRP, lambda s: four_copy(s).start(), 1)
    own_sums = pltpu.make_async_copy(ag1b, ag2.at[grp], out_sem.at[2])
    own_sums.start()

    def take_back(j):
        back_arrival(j).wait_recv()
        peer = near_peer(j)
        for k in range(4):
            value = chain[ids_s[9 + k, peer]]
            tiles = from_face(returned[j, k])
            for q in range(4):
                chain[4 * j + k, :, 128 * q : 128 * q + 128] = value[:, 128 * q : 128 * q + 128] + tiles[q]

    loop(NEAR, take_back, unroll=3)

    face_sums = [term[ids_s[8, f]] + chain[ids_s[13, f]] for f in range(LOCAL)]

    def tile_of(f, q):
        return face_sums[f][:, 128 * q : 128 * q + 128]

    for b in range(4):
        for f, row in ((2, 0), (3, 7)):
            for q in range(4):
                yrim[pl.ds(q * 256 + b * 8 + row, 8, stride=32), :] = tile_of(6 * b + f, q)
        for y in range(8):
            below, above = tile_of(6 * b + 4, y // 2), tile_of(6 * b + 5, y // 2)
            if y % 2 == 0:
                value = jnp.where(low8, below, half(above))
            else:
                value = jnp.where(low8, half(below), above)
            zrim[pl.ds(b * 8 + y, 8, stride=32), :] = value
    edge = jnp.logical_or(row8 == 0, row8 == 7)
    for b in range(4):
        for x in range(8):
            at = 32 * x + 8 * b
            rim_z = zrim[at : at + 8, :]
            tiles = []
            for q in range(4):
                value = inner[256 * q + at : 256 * q + at + 8, :]
                if x == 0 or x == 7:
                    value = value + tile_of(6 * b + (0 if x == 0 else 1), q)
                value = value + jnp.where(edge, yrim[256 * q + at : 256 * q + at + 8, :], 0.0)
                if q == 0:
                    value = value + jnp.where(low8, rim_z, 0.0)
                if q == 3:
                    value = value + jnp.where(low8, 0.0, rim_z)
                tiles.append(value)
            grad[b, x] = jnp.concatenate(tiles, axis=1).astype(BF16)
    grad_store = pltpu.make_async_copy(grad, grad_h, out_sem.at[1])
    grad_store.start()

    own_sums.wait()
    four_all.wait_recv()

    for group in (key_all, tg_all, tile_all, one_all, two_all, three_all, four_all):
        group.wait_send()
    pltpu.make_async_remote_copy(
        src_ref=sbuf, dst_ref=returned, send_sem=face_sem.at[2], recv_sem=face_sem.at[1],
        device_id=(me + 1) & (PEERS - 1), device_id_type=LOGICAL,
    ).wait_send()
    for store in (coarse_store, grad_store):
        store.wait()


def finish_kernel(
    coarse, grad, sums, coarse_o, grad_o, conv_o, down_o, coarse_v, grad_v, ag2, conv_v, down_v, loaded, sems
):
    loads = [
        pltpu.make_async_copy(source, target, loaded.at[i])
        for i, (source, target) in enumerate(((sums, ag2), (coarse, coarse_v), (grad, grad_v)))
    ]
    for load in loads:
        load.start()
    for load in loads:
        load.wait()
    stores = [
        pltpu.make_async_copy(coarse_v, coarse_o, sems.at[0]), pltpu.make_async_copy(grad_v, grad_o, sems.at[1])
    ]
    for store in stores:
        store.start()
    got = [ag2[g].astype(F32) for g in range(N_GRP)]

    def save(source, target, number):
        stores.append(pltpu.make_async_copy(source, target, sems.at[number]))
        stores[-1].start()

    for s in range(15):
        value = jnp.concatenate([got[g][8 * s : 8 * s + 8] for g in range(N_GRP)], axis=0)
        if s == 14:
            down_v[...] = value
            save(down_v, down_o, 6)
            continue
        turned = value.T
        conv_v[2 * s] = turned[0:64]
        if s < 13:
            conv_v[2 * s + 1] = turned[64:128]
        if s in (3, 6, 9, 13):
            first, last = {3: (0, 8), 6: (8, 14), 9: (14, 20), 13: (20, 27)}[s]
            part = pl.ds(first, last - first)
            save(conv_v.at[part], conv_o.at[part], {3: 2, 6: 3, 9: 4, 13: 5}[s])
    for store in stores:
        store.wait()


def dma(*shape):
    return pltpu.SemaphoreType.DMA(shape)


def per_device(features, conv_weight, down_weight, cotangent, src_table, send_list, child_map):
    hbm = pl.BlockSpec(memory_space=pl.ANY)
    vmem, smem, i32 = pltpu.VMEM, pltpu.SMEM, jnp.int32
    coarse, grad_input, sums = pl.pallas_call(
        block_kernel,
        out_shape=(
            jax.ShapeDtypeStruct((1, 512, 128), BF16),
            jax.ShapeDtypeStruct((4, 8, 8, 512), BF16),
            jax.ShapeDtypeStruct((N_GRP, 128, 128), BF16),
        ),
        in_specs=[hbm] * 6 + [pl.BlockSpec(memory_space=pltpu.SMEM)],
        out_specs=(hbm,) * 3,
        scratch_shapes=[
            vmem((4, 8, 8, 512), BF16), vmem((27, C, C), BF16), vmem((C, 128), BF16), vmem((1, 512, 128), BF16),
            smem((4, 26), i32), vmem((4, 26), i32), vmem((8, 128), i32),
            smem((4, PEERS), i32), vmem((4, PEERS), i32), vmem((16, 128), i32), smem((16, 128), i32),
            vmem((1024, 128), F32),
            vmem((LOCAL, 16, 256), BF16),
            vmem((TABLE, 16, 256), BF16),
            vmem((NEAR, 4, 16, 256), BF16),
            vmem((NEAR, 4, 16, 256), BF16),
            vmem((8, 128), i32), vmem((N_SUB, 8, 128), i32),
            vmem((128, 128), BF16),
            vmem((N_SUB, 32, 128), BF16), vmem((N_SUB, 32, 128), BF16),
            vmem((512, 512), BF16),
            vmem((9, 256, 128), BF16), vmem((9, 128, 256), BF16),
            vmem((256, 128), F32), vmem((1280, 128), F32),
            vmem((3, 320, 640), BF16),
            vmem((1024, 128), F32),
            vmem((384, 768), BF16),
            vmem((128, 1024), BF16),
            vmem((15 * 320, 128), F32),
            vmem((TERMS + 1, 8, 512), F32),
            vmem((1024, 128), F32),
            vmem((32, 128), BF16), vmem((N_SUB, 32, 128), BF16),
            vmem((N_GRP, 128, 128), F32), vmem((N_GRP, 128, 128), BF16), vmem((N_GRP, 128, 128), BF16),
            vmem((128, 128), F32),
            vmem((N_SUB, 8, 128), F32), vmem((8, 128), F32), vmem((N_SUB, 8, 128), F32),
            vmem((128, 128), BF16),
            vmem((SLOTS + 1, 8, 512), F32),
            vmem((1, 512, 128), BF16), vmem((4, 8, 8, 512), BF16),
        ]
        + [dma(3), dma(NEAR)]
        + [dma(2)] * 7
        + [dma(9), dma(3)],
        compiler_params=pltpu.CompilerParams(
            collective_id=0, has_side_effects=True, vmem_limit_bytes=VMEM_LIMIT
        ),
        name="block",
    )(features, conv_weight, down_weight, cotangent, src_table, send_list[0].T, child_map)
    return pl.pallas_call(
        finish_kernel,
        out_shape=(
            jax.ShapeDtypeStruct((1, 512, 128), BF16),
            jax.ShapeDtypeStruct((4, 8, 8, 512), BF16),
            jax.ShapeDtypeStruct((27, C, C), F32),
            jax.ShapeDtypeStruct((C, 128), F32),
        ),
        in_specs=[hbm] * 3,
        out_specs=(hbm,) * 4,
        scratch_shapes=[
            vmem((1, 512, 128), BF16), vmem((4, 8, 8, 512), BF16),
            vmem((N_GRP, 128, 128), BF16), vmem((27, C, C), F32), vmem((C, 128), F32), dma(3), dma(7),
        ],
        compiler_params=pltpu.CompilerParams(vmem_limit_bytes=VMEM_LIMIT),
        name="finish",
    )(coarse, grad_input, sums)


def solution(mesh):
    both = ("grp", "sub")
    placed = (
        P(both, None, None, None),
        P(),
        P(),
        P(both, None, None),
        P(both, None),
        P(both, None, None),
        P(both),
    )
    return jax.shard_map(
        per_device,
        mesh=mesh,
        in_specs=placed,
        out_specs=(P(both, None, None), P(both, None, None, None), P(), P()),
        check_vma=False,
    )
```

```python
import jax
import jax.numpy as jnp
from jax import lax
from jax.experimental import pallas as pl
from jax.experimental.pallas import tpu as pltpu
from jax.sharding import PartitionSpec as P

LOGICAL = pl.DeviceIdType.LOGICAL
N_GRP, N_SUB = 8, 16
PEERS = N_GRP * N_SUB
NEAR = 33
C = 64
F32, BF16 = jnp.float32, jnp.bfloat16
LOCAL = 24
DUMP = LOCAL + 4 * NEAR
TABLE = DUMP + 4
VMEM_LIMIT = 58 * 1024 * 1024
TERMS = 4 * 26
FIRST_FACES = NEAR
CUTS = (7, 18)
SLOTS = 4 * NEAR

OFFSETS = [
    (x, y, z)
    for x in (-1, 0, 1)
    for y in (-1, 0, 1)
    for z in (-1, 0, 1)
    if (x, y, z) != (0, 0, 0)
]
NUMBER = {offset: number for number, offset in enumerate(OFFSETS)}


def step_of(j):
    return jnp.where(j < 16, j + 1, jnp.where(j == 16, 64, j + 95))


def twin(j):
    return NEAR - 1 - j


def near_of(step):
    return jnp.where(step <= 16, step - 1, jnp.where(step == 64, 16, step - 95))


def lane_iota(rows):
    return lax.broadcasted_iota(jnp.int32, (rows, 128), 1)


def row_iota(rows):
    return lax.broadcasted_iota(jnp.int32, (rows, 128), 0)


def half(tile):
    return pltpu.roll(tile, 64, axis=1)


def lows(rows):
    return lane_iota(rows) < 64


def to_face(tiles):
    top = jnp.concatenate([tiles[0], tiles[1]], axis=1)
    bottom = jnp.concatenate([tiles[2], tiles[3]], axis=1)
    return jnp.concatenate([top, bottom], axis=0)


def from_face(face):
    face = face.astype(F32)
    return [face[0:8, 0:128], face[0:8, 128:256], face[8:16, 0:128], face[8:16, 128:256]]


def widen(tiles, below, above):
    low = lows(tiles[0].shape[0])
    rolled = [half(tile) for tile in tiles]
    result = [jnp.where(low, half(below), rolled[0])]
    for m in range(1, 4):
        result.append(jnp.where(low, rolled[m - 1], rolled[m]))
    result.append(jnp.where(low, rolled[3], half(above)))
    return result


def narrow(tiles):
    low = lows(tiles[0].shape[0])
    rolled = [half(tile) for tile in tiles]
    return [jnp.where(low, rolled[q], rolled[q + 1]) for q in range(4)]


def roll8(value, shift):
    rows = value.shape[0]
    grouped = value.reshape(rows // 8, 8, 128)
    return pltpu.roll(grouped, shift % 8, axis=1).reshape(rows, 128)

def loop(count, body, start=0, unroll=True):
    def step(i, _):
        body(i)
        return 0

    lax.fori_loop(start, count, step, 0, unroll=unroll)


def column_max(value):
    best = value[0:8]
    for i in range(1, 16):
        best = jnp.maximum(best, value[8 * i : 8 * i + 8])
    for shift in (4, 2, 1):
        best = jnp.maximum(best, pltpu.roll(best, shift, axis=0))
    return best


def index_tables(src_v, send_v, ids, me):
    whole = (128, 128)
    below = lax.broadcasted_iota(jnp.int32, whole, 0)
    along = lax.broadcasted_iota(jnp.int32, whole, 1)
    rows = [jnp.broadcast_to(src_v[b : b + 1, :], whole) for b in range(4)]
    columns = [row.T for row in rows]

    def pick(cases, none):
        best = None
        for match, value in cases:
            value = jnp.where(match, value, -1)
            best = value if best is None else jnp.maximum(best, value)
        best = column_max(best)
        return jnp.where(best < 0, none, best)[0:1]

    for b in range(4):
        cases = []
        for c in range(b + 1):
            match = jnp.logical_and(columns[c] == rows[b], columns[c] >= 0)
            if c == b:
                match = jnp.logical_and(match, below < along)
            cases.append((match, 26 * c + below))
        ids[b : b + 1, :] = pick(cases, TERMS)
    for k in range(4):
        code = jnp.where(along < NEAR, LOCAL + 4 * ((me + step_of(along)) & (PEERS - 1)) + k, -5)
        ids[4 + k : 5 + k, :] = pick([(columns[b] == code, 26 * b + below) for b in range(4)], TERMS)
    code = jnp.where(along < LOCAL, along, -5)
    ids[8:9, :] = pick([(columns[b] == code, 26 * b + below) for b in range(4)], TERMS)

    def number(device):
        return 4 * jnp.clip(near_of((device - me) & (PEERS - 1)), 0, NEAR - 1)

    rows = [jnp.broadcast_to(send_v[k : k + 1, :], whole) for k in range(4)]
    columns = [row.T for row in rows]
    first, second = number(below), number(along)
    for k in range(4):
        cases = []
        for c in range(4):
            match = jnp.logical_and(columns[c] == rows[k], columns[c] >= 0)
            cases.append((jnp.logical_and(match, first + c < second + k), first + c))
        ids[9 + k : 10 + k, :] = pick(cases, SLOTS)
    ids[13:14, :] = pick([(columns[c] == along, first + c) for c in range(4)], SLOTS)


def block_kernel(
    feat_h, cw_h, dw_h, cot_h, src_h, send_h, child_s,
    coarse_h, grad_h, ag2,
    feat, cw, dw, cot, src_s, src_p, src_v, send_s, send_v, ids, ids_s,
    flat, faces, table, sbuf, returned, key_s, key_r, dwp, tg_s, tg_r, place,
    band, bandt, zrim, yrim, pad, pre, pg, pgt, acc_a, term, inner,
    tile_s, tile_r, convt, convb, rs1, tot, rs2, fin, ag1, ag1b, chain, coarse, grad,
    face_sem, back_rs, key_sem, tg_sem, tile_sem, one_sem, two_sem, three_sem, four_sem, in_sem, out_sem,
):
    grp, sub = lax.axis_index("grp"), lax.axis_index("sub")
    me = grp * N_SUB + sub

    barrier = pltpu.get_barrier_semaphore()

    def signal(peer):
        pl.semaphore_signal(barrier, inc=1, device_id=peer, device_id_type=LOGICAL)

    def near_peer(j):
        return (me + step_of(j)) & (PEERS - 1)

    loop(NEAR, lambda j: signal(near_peer(j)))
    for far in (2, 3, 5, 6):
        signal(((grp + far) & (N_GRP - 1)) * N_SUB + sub)

    loads = [
        pltpu.make_async_copy(source, target, in_sem.at[i])
        for i, (source, target) in enumerate(
            (
                (feat_h, feat), (send_h, send_s), (send_h, send_v), (cw_h, cw), (cot_h, cot), (dw_h, dw),
                (src_h, src_s), (src_h, src_p),
            )
        )
    ]
    for load in loads:
        load.start()
    loads[0].wait()

    low8, row8 = lows(8), row_iota(8)
    for b in range(4):
        for x in range(8):
            v = feat[b, x].astype(F32)
            for q in range(4):
                flat[q * 256 + b * 64 + x * 8 : q * 256 + b * 64 + x * 8 + 8, :] = v[:, 128 * q : 128 * q + 128]

    def rows(q, b, y):
        return flat[pl.ds(q * 256 + b * 64 + y, 8, stride=8), :]

    def face(number, tiles):
        value = to_face(tiles).astype(BF16)
        faces[number] = value
        table[number] = value

    for b in range(4):
        for s, x in ((0, 0), (1, 7)):
            v = feat[b, x].astype(F32)
            face(b * 6 + s, [v[:, 128 * q : 128 * q + 128] for q in range(4)])
        for s, y in ((2, 0), (3, 7)):
            face(b * 6 + s, [rows(q, b, y) for q in range(4)])
        first = [rows(0, b, y) for y in range(8)]
        last = [rows(3, b, y) for y in range(8)]
        face(b * 6 + 4, [jnp.where(low8, first[2 * q], half(first[2 * q + 1])) for q in range(4)])
        face(b * 6 + 5, [jnp.where(low8, half(last[2 * q]), last[2 * q + 1]) for q in range(4)])
    table[DUMP] = jnp.zeros((16, 256), BF16)
    for b in range(4):
        key_s[b : b + 1] = jnp.full((1, 128), 8 * child_s[b], jnp.int32)
    loads[1].wait()

    def pack(j):
        peer = near_peer(j)
        for k in range(4):
            sbuf[j, k] = faces[jnp.maximum(send_s[k, peer], 0)]

    loop(NEAR, pack)
    key_s[4:8] = jnp.zeros((4, 128), jnp.int32)
    key_r[sub] = key_s[...]
    pl.semaphore_wait(barrier, NEAR + 4)

    def sub_copy(s, src, dst, sems):
        other = (sub + s) & (N_SUB - 1)
        return pltpu.make_async_remote_copy(
            src_ref=src(other), dst_ref=dst.at[sub], send_sem=sems.at[0], recv_sem=sems.at[1],
            device_id=grp * N_SUB + other, device_id_type=LOGICAL,
        )

    def grp_copy(s, src, dst, sems):
        other = (grp + s) & (N_GRP - 1)
        return pltpu.make_async_remote_copy(
            src_ref=src(other), dst_ref=dst(grp), send_sem=sems.at[0], recv_sem=sems.at[1],
            device_id=other * N_SUB + sub, device_id_type=LOGICAL,
        )

    def near_copy(j, dst, send_sem, recv_sem):
        return pltpu.make_async_remote_copy(
            src_ref=sbuf.at[j], dst_ref=dst, send_sem=send_sem, recv_sem=recv_sem,
            device_id=near_peer(j), device_id_type=LOGICAL,
        )

    def all_of(ref, sems):
        return pltpu.make_async_remote_copy(
            src_ref=ref, dst_ref=ref, send_sem=sems.at[0], recv_sem=sems.at[1],
            device_id=(me + 1) & (PEERS - 1), device_id_type=LOGICAL,
        )

    def key_copy(s):
        return sub_copy(s, lambda other: key_s, key_r, key_sem)

    def tg_copy(s):
        return sub_copy(s, lambda other: tg_s.at[other], tg_r, tg_sem)

    def tile_copy(s):
        return sub_copy(s, lambda other: tile_s, tile_r, tile_sem)

    def face_copy(j):
        return near_copy(j, table.at[pl.ds(LOCAL + 4 * twin(j), 4)], face_sem.at[0], face_sem.at[1])

    def back_copy(j):
        return near_copy(j, returned.at[twin(j)], face_sem.at[2], back_rs.at[twin(j)])

    def back_arrival(j):
        return near_copy(j, returned.at[j], face_sem.at[2], back_rs.at[j])

    def one_copy(s):
        return grp_copy(s, lambda other: convb.at[other], lambda slot: rs1.at[slot], one_sem)

    def two_copy(s):
        return sub_copy(s, lambda other: tot.at[pl.ds(8 * other, 8)], rs2, two_sem)

    def three_copy(s):
        return sub_copy(s, lambda other: fin, ag1, three_sem)

    def four_copy(s):
        return grp_copy(s, lambda other: ag1b, lambda slot: ag2.at[slot], four_sem)

    sub_all, grp_all = pl.ds(0, N_SUB - 1), pl.ds(0, N_GRP - 1)
    key_all = all_of(key_r.at[sub_all], key_sem)
    tg_all = all_of(tg_r.at[sub_all], tg_sem)
    tile_all = all_of(tile_r.at[sub_all], tile_sem)
    face_all = all_of(table.at[pl.ds(LOCAL, SLOTS)], face_sem)
    one_all = all_of(rs1.at[grp_all], one_sem)
    two_all = all_of(rs2.at[sub_all], two_sem)
    three_all = all_of(ag1.at[sub_all], three_sem)
    four_all = all_of(ag2.at[grp_all], four_sem)

    loop(N_SUB, lambda s: key_copy(s).start(), 1)
    loop(FIRST_FACES, lambda j: face_copy(j).start())

    for load in loads[2:]:
        load.wait()
    band[...] = jnp.zeros_like(band)
    bandt[...] = jnp.zeros_like(bandt)
    for n in range(9):
        for s in range(3):
            w = cw[3 * n + s]
            band[n, 64 * s : 64 * s + 64, 0:64] = w
            band[n, 64 * s + 64 : 64 * s + 128, 64:128] = w
            d = 2 - s
            bandt[n, 0:64, 64 * d : 64 * d + 64] = w
            bandt[n, 64:128, 64 * d + 64 : 64 * d + 128] = w
    pg[...] = jnp.zeros_like(pg)
    term[TERMS] = jnp.zeros((8, 512), F32)
    chain[SLOTS] = jnp.zeros((8, 512), F32)
    dwp[0:64] = dw[...]
    dwp[64:128] = dw[...]
    def voxel_key(shape, dim):
        v = lax.broadcasted_iota(jnp.int32, shape, dim)
        x, y, z = v >> 6, (v >> 3) & 7, v & 7
        spot = 16 * (x >> 1) + 4 * (y >> 1) + (z >> 1)
        inside = 4 * (x & 1) + 2 * (y & 1) + (z & 1)
        return (64 * sub + spot) * 8 + inside

    key_all.wait_recv()
    ijk = row_iota(8)
    keys = jnp.concatenate(
        [jnp.broadcast_to(key_r[s, b : b + 1, :], (8, 128)) + ijk for s in range(N_SUB) for b in range(4)], axis=0
    )
    wanted = jnp.broadcast_to(voxel_key((1, 512), 1), (512, 512))
    take = jnp.where(jnp.concatenate([keys] * 4, axis=1) == wanted, 1.0, 0.0).astype(BF16)
    tiles = jnp.dot(take, cot[0], preferred_element_type=F32).astype(BF16)
    tg_s[...] = tiles.reshape(N_SUB, 32, 128)
    tg_r[sub] = tg_s[sub]
    loop(N_SUB, lambda s: tg_copy(s).start(), 1)
    loop(NEAR, lambda j: face_copy(j).start(), FIRST_FACES)
    key_row = jnp.concatenate([keys[128 * q : 128 * q + 128].T for q in range(4)], axis=1)[0:1]
    place[...] = jnp.where(
        jnp.broadcast_to(key_row, (512, 512)) == jnp.broadcast_to(voxel_key((512, 1), 0), (512, 512)), 1.0, 0.0
    ).astype(BF16)
    src_v[...] = jnp.full((8, 128), -1, jnp.int32)
    src_v[0:4, 0:26] = src_p[...]
    index_tables(src_v, send_v, ids, me)
    to_scalars = pltpu.make_async_copy(ids, ids_s, in_sem.at[8])
    to_scalars.start()
    to_scalars.wait()
    face_all.wait_recv()

    def slab(b, offset):
        code = src_s[b, NUMBER[offset]]
        remote = code - LOCAL
        spot = LOCAL + 4 * near_of(((remote >> 2) - me) & (PEERS - 1)) + (remote & 3)
        return from_face(table[jnp.where(code < 0, DUMP, jnp.where(code < LOCAL, code, spot))])

    for b in range(4):
        below, above = slab(b, (0, 0, -1)), slab(b, (0, 0, 1))
        for y in range(8):
            q = y // 2
            if y % 2 == 0:
                value = jnp.where(low8, above[q], half(below[q]))
            else:
                value = jnp.where(low8, half(above[q]), below[q])
            zrim[pl.ds(b * 8 + y, 8, stride=32), :] = value
        for dy, row in ((-1, 7), (1, 0)):
            wide = widen(slab(b, (0, dy, 0)), slab(b, (0, dy, -1))[3], slab(b, (0, dy, 1))[0])
            for m in range(5):
                yrim[pl.ds(m * 256 + b * 8 + row, 8, stride=32), :] = wide[m]

    def put(m, first, value, before, after):
        count = value.shape[0]
        lanes = slice(128 * m, 128 * m + 128)
        row = row_iota(count) & 7
        pad[1, first : first + count, lanes] = value.astype(BF16)
        pad[0, first : first + count, lanes] = roll8(jnp.where(row == 7, before, value), 1).astype(BF16)
        pad[2, first : first + count, lanes] = roll8(jnp.where(row == 0, after, value), -1).astype(BF16)

    for dx, plane in ((-1, 0), (1, 9)):
        parts = [[], [], []]
        for b in range(4):
            for i, dy in enumerate((-1, 0, 1)):
                parts[i].append(
                    widen(slab(b, (dx, dy, 0)), slab(b, (dx, dy, -1))[3], slab(b, (dx, dy, 1))[0])
                )
        for m in range(5):
            before, value, after = [
                jnp.concatenate([part[b][m] for b in range(4)], axis=0) for part in parts
            ]
            put(m, plane * 32, value, before, after)
    for x in range(8):
        inside = []
        for q in range(4):
            inside.append(
                jnp.concatenate([feat[b, x][:, 128 * q : 128 * q + 128].astype(F32) for b in range(4)], axis=0)
            )
        rim = zrim[32 * x : 32 * x + 32, :]
        wide = widen(inside, rim, rim)
        for m in range(5):
            edge = yrim[m * 256 + 32 * x : m * 256 + 32 * x + 32, :]
            put(m, 32 * x + 32, wide[m], edge, edge)

    for m in range(4):
        total = None
        for n in range(9):
            sx, sy = n // 3, n % 3
            product = jnp.dot(
                pad[sy, 32 * sx : 32 * sx + 256, 128 * m : 128 * m + 256], band[n], preferred_element_type=F32
            )
            total = product if total is None else total + product
        pre[256 * m : 256 * m + 256] = total

    tg_all.wait_recv()
    grad_tile = tg_r[0].astype(F32)
    for s in range(1, N_SUB):
        grad_tile += tg_r[s].astype(F32)
    cot_rows = grad_tile.astype(BF16)
    grad_tile = (
        lax.dot_general(cot_rows, dwp[...], (((1,), (1,)), ((), ())), preferred_element_type=F32)
        .astype(BF16)
        .astype(F32)
        .reshape(4, 8, 128)
    )
    sub_row = lax.broadcasted_iota(jnp.int32, (4, 8, 128), 1)
    pooled = jnp.zeros((4, 8, 128), F32)
    for top in range(2):
        for deep in range(2):
            spread = jnp.where(
                sub_row < 4,
                jnp.broadcast_to(grad_tile[:, 4 * top + deep : 4 * top + deep + 1, :], (4, 8, 128)),
                jnp.broadcast_to(grad_tile[:, 4 * top + 2 + deep : 4 * top + 3 + deep, :], (4, 8, 128)),
            ).reshape(32, 128) * (1.0 / 64.0)
            total = jnp.zeros((32, 128), F32)
            for m in (2 * deep, 2 * deep + 1):
                for x in range(4 * top, 4 * top + 4):
                    u = pre[256 * m + 32 * x : 256 * m + 32 * x + 32, :]
                    g = 1.0 / (1.0 + jnp.exp(-u))
                    total += u * g
                    slope = g * (1.0 + u * (1.0 - g))
                    pg[64 + 32 * x : 96 + 32 * x, 128 * m + 128 : 128 * m + 256] = (spread * slope).astype(BF16)
            total = total + half(total)
            grouped = total.reshape(4, 8, 128)
            grouped = grouped + pltpu.roll(grouped, 7, axis=1)
            grouped = grouped + pltpu.roll(grouped, 6, axis=1)
            for mid in range(2):
                pooled = jnp.where(
                    sub_row == 4 * top + 2 * mid + deep,
                    jnp.broadcast_to(grouped[:, 4 * mid : 4 * mid + 1, :], (4, 8, 128)),
                    pooled,
                )
    pooled = pooled.reshape(32, 128) * (1.0 / 64.0)
    pooled = jnp.where(lows(32), pooled, 0.0)
    tile_s[...] = pooled.astype(BF16)
    down = jnp.dot(pooled.T.astype(BF16), cot_rows, preferred_element_type=F32)
    for g in range(N_GRP):
        convt[g, 112:120] = down[8 * g : 8 * g + 8]
        convt[g, 120:128] = jnp.zeros((8, 128), F32)
    tile_r[sub] = tile_s[...]
    loop(N_SUB, lambda s: tile_copy(s).start(), 1)

    for m in range(4):
        pgt[:, 256 * m : 256 * m + 256] = (
            pg[64:320, 128 * m + 128 : 128 * m + 256].astype(F32).T.astype(BF16)
        )
    low64 = lows(64)

    def keep(chunk, value):
        for g in range(N_GRP):
            convt[g, 8 * chunk : 8 * chunk + 8] = value[8 * g : 8 * g + 8]

    held = None
    for n in range(9):
        sx, sy = n // 3, n % 3
        total = None
        for m in range(4):
            product = jnp.dot(
                pgt[:, 256 * m : 256 * m + 256],
                pad[sy, 32 * sx : 32 * sx + 256, 128 * m : 128 * m + 256],
                preferred_element_type=F32,
            )
            total = product if total is None else total + product
        r0, r1 = half(total[64:128, 0:128]), half(total[64:128, 128:256])
        first = total[0:64, 0:128] + jnp.where(low64, r0, r1)
        second = total[0:64, 128:256] + r1
        at = 3 * (n // 2)
        if n % 2 == 0:
            keep(at, first)
            held = second
        else:
            turned = half(first)
            keep(at + 1, jnp.where(low64, held, turned))
            keep(at + 2, jnp.where(low64, turned, half(second)))
    keep(13, jnp.where(low64, held, 0.0))
    convb[...] = convt[...].astype(BF16)
    rs1[grp] = jnp.zeros((128, 128), BF16)
    loop(N_GRP, lambda s: one_copy(s).start(), 1)

    for sy in range(3):
        for m in range(5):
            total = None
            for sx in range(3):
                product = lax.dot_general(
                    pg[32 * (2 - sx) : 32 * (2 - sx) + 320, 128 * m : 128 * m + 256],
                    bandt[3 * sx + sy],
                    (((1,), (1,)), ((), ())),
                    preferred_element_type=F32,
                )
                total = product if total is None else total + product
            acc_a[(sy * 5 + m) * 320 : (sy * 5 + m) * 320 + 320, :] = total

    def part(sy, m, first, count):
        return acc_a[(sy * 5 + m) * 320 + first : (sy * 5 + m) * 320 + first + count, :]

    def middle(m, first, count):
        row = row_iota(count) & 7
        return (
            part(1, m, first, count)
            + jnp.where(row < 7, roll8(part(0, m, first, count), -1), 0.0)
            + jnp.where(row > 0, roll8(part(2, m, first, count), 1), 0.0)
        )

    for x in range(8):
        wide = [middle(m, 32 * x + 32, 32) for m in range(5)]
        for q, tile in enumerate(narrow(wide)):
            inner[256 * q + 32 * x : 256 * q + 32 * x + 32, :] = tile
        zrim[32 * x : 32 * x + 32, :] = jnp.where(lows(32), wide[0], wide[4])

    planes = {}
    for dx, plane in ((-1, 0), (1, 9)):
        for b in range(4):
            first = 32 * plane + 8 * b
            planes[dx, 0, b] = [middle(m, first, 8) for m in range(5)]
            planes[dx, -1, b] = [
                jnp.where(row8 == 7, roll8(part(0, m, first, 8), -1), 0.0) for m in range(5)
            ]
            planes[dx, 1, b] = [
                jnp.where(row8 == 0, roll8(part(2, m, first, 8), 1), 0.0) for m in range(5)
            ]

    def rim(b, offset):
        dx, dy, dz = offset
        if dx == 0 and dy == 0:
            rims = [zrim[pl.ds(b * 8 + y, 8, stride=32), :] for y in range(8)]
            if dz < 0:
                return [jnp.where(low8, rims[2 * q], half(rims[2 * q + 1])) for q in range(4)]
            return [jnp.where(low8, half(rims[2 * q]), rims[2 * q + 1]) for q in range(4)]
        if dx != 0:
            wide = planes[dx, dy, b]
        else:
            sy, row = (0, 0) if dy < 0 else (2, 7)
            wide = [
                acc_a[pl.ds((sy * 5 + m) * 320 + 32 + b * 8 + row, 8, stride=32), :] for m in range(5)
            ]
        if dz == 0:
            return narrow(wide)
        if dz > 0:
            return [jnp.where(low8, half(wide[4]), 0.0), None, None, None]
        return [None, None, None, jnp.where(low8, 0.0, half(wide[0]))]

    for b in range(4):
        for t, offset in enumerate(OFFSETS):
            earlier = ids_s[b, t]
            for q, tile in enumerate(rim(b, offset)):
                value = term[earlier, :, 128 * q : 128 * q + 128]
                term[26 * b + t, :, 128 * q : 128 * q + 128] = value if tile is None else value + tile

    face_all.wait_send()

    def leave(j):
        for k in range(4):
            value = term[ids_s[4 + k, j]]
            sbuf[j, k] = to_face([value[:, 128 * q : 128 * q + 128] for q in range(4)]).astype(BF16)
        back_copy(j).start()

    loop(CUTS[0], leave)

    one_all.wait_recv()
    total = convt[grp]
    for g in range(N_GRP):
        total += rs1[g].astype(F32)
    tot[...] = total
    loop(N_SUB, lambda s: two_copy(s).start(), 1)
    loop(CUTS[1], leave, CUTS[0])
    rs2[sub] = tot[pl.ds(pl.multiple_of(8 * sub, 8), 8), :]
    two_all.wait_recv()
    total = rs2[0]
    for s in range(1, N_SUB):
        total += rs2[s]
    fin[...] = total
    loop(N_SUB, lambda s: three_copy(s).start(), 1)
    loop(NEAR, leave, CUTS[1])

    tile_all.wait_recv()
    coarse_in = jnp.dot(place[...], tile_r[...].reshape(512, 128), preferred_element_type=F32)
    dwp[64:128] = jnp.zeros((64, 128), BF16)
    coarse[0] = jnp.dot(coarse_in.astype(BF16), dwp[...], preferred_element_type=F32).astype(BF16)
    coarse_store = pltpu.make_async_copy(coarse, coarse_h, out_sem.at[0])
    coarse_store.start()
    ag1[sub] = fin[...]
    three_all.wait_recv()
    ag1b[...] = ag1[...].reshape(128, 128).astype(BF16)
    loop(N_GRP, lambda s: four_copy(s).start(), 1)
    own_sums = pltpu.make_async_copy(ag1b, ag2.at[grp], out_sem.at[2])
    own_sums.start()

    def take_back(j):
        back_arrival(j).wait_recv()
        peer = near_peer(j)
        for k in range(4):
            value = chain[ids_s[9 + k, peer]]
            tiles = from_face(returned[j, k])
            for q in range(4):
                chain[4 * j + k, :, 128 * q : 128 * q + 128] = value[:, 128 * q : 128 * q + 128] + tiles[q]

    loop(NEAR, take_back, unroll=3)

    face_sums = [term[ids_s[8, f]] + chain[ids_s[13, f]] for f in range(LOCAL)]

    def tile_of(f, q):
        return face_sums[f][:, 128 * q : 128 * q + 128]

    for b in range(4):
        for f, row in ((2, 0), (3, 7)):
            for q in range(4):
                yrim[pl.ds(q * 256 + b * 8 + row, 8, stride=32), :] = tile_of(6 * b + f, q)
        for y in range(8):
            below, above = tile_of(6 * b + 4, y // 2), tile_of(6 * b + 5, y // 2)
            if y % 2 == 0:
                value = jnp.where(low8, below, half(above))
            else:
                value = jnp.where(low8, half(below), above)
            zrim[pl.ds(b * 8 + y, 8, stride=32), :] = value
    edge = jnp.logical_or(row8 == 0, row8 == 7)
    for b in range(4):
        for x in range(8):
            at = 32 * x + 8 * b
            rim_z = zrim[at : at + 8, :]
            tiles = []
            for q in range(4):
                value = inner[256 * q + at : 256 * q + at + 8, :]
                if x == 0 or x == 7:
                    value = value + tile_of(6 * b + (0 if x == 0 else 1), q)
                value = value + jnp.where(edge, yrim[256 * q + at : 256 * q + at + 8, :], 0.0)
                if q == 0:
                    value = value + jnp.where(low8, rim_z, 0.0)
                if q == 3:
                    value = value + jnp.where(low8, 0.0, rim_z)
                tiles.append(value)
            grad[b, x] = jnp.concatenate(tiles, axis=1).astype(BF16)
    grad_store = pltpu.make_async_copy(grad, grad_h, out_sem.at[1])
    grad_store.start()

    own_sums.wait()
    four_all.wait_recv()

    for group in (key_all, tg_all, tile_all, one_all, two_all, three_all, four_all):
        group.wait_send()
    pltpu.make_async_remote_copy(
        src_ref=sbuf, dst_ref=returned, send_sem=face_sem.at[2], recv_sem=face_sem.at[1],
        device_id=(me + 1) & (PEERS - 1), device_id_type=LOGICAL,
    ).wait_send()
    for store in (coarse_store, grad_store):
        store.wait()


def finish_kernel(
    coarse, grad, sums, coarse_o, grad_o, conv_o, down_o, coarse_v, grad_v, ag2, conv_v, down_v, loaded, sems
):
    loads = [
        pltpu.make_async_copy(source, target, loaded.at[i])
        for i, (source, target) in enumerate(((sums, ag2), (coarse, coarse_v), (grad, grad_v)))
    ]
    for load in loads:
        load.start()
    for load in loads:
        load.wait()
    stores = [
        pltpu.make_async_copy(coarse_v, coarse_o, sems.at[0]), pltpu.make_async_copy(grad_v, grad_o, sems.at[1])
    ]
    for store in stores:
        store.start()
    got = [ag2[g].astype(F32) for g in range(N_GRP)]

    def save(source, target, number):
        stores.append(pltpu.make_async_copy(source, target, sems.at[number]))
        stores[-1].start()

    for s in range(15):
        value = jnp.concatenate([got[g][8 * s : 8 * s + 8] for g in range(N_GRP)], axis=0)
        if s == 14:
            down_v[...] = value
            save(down_v, down_o, 6)
            continue
        turned = value.T
        conv_v[2 * s] = turned[0:64]
        if s < 13:
            conv_v[2 * s + 1] = turned[64:128]
        if s in (3, 6, 9, 13):
            first, last = {3: (0, 8), 6: (8, 14), 9: (14, 20), 13: (20, 27)}[s]
            part = pl.ds(first, last - first)
            save(conv_v.at[part], conv_o.at[part], {3: 2, 6: 3, 9: 4, 13: 5}[s])
    for store in stores:
        store.wait()


def dma(*shape):
    return pltpu.SemaphoreType.DMA(shape)


def per_device(features, conv_weight, down_weight, cotangent, src_table, send_list, child_map):
    hbm = pl.BlockSpec(memory_space=pl.ANY)
    vmem, smem, i32 = pltpu.VMEM, pltpu.SMEM, jnp.int32
    coarse, grad_input, sums = pl.pallas_call(
        block_kernel,
        out_shape=(
            jax.ShapeDtypeStruct((1, 512, 128), BF16),
            jax.ShapeDtypeStruct((4, 8, 8, 512), BF16),
            jax.ShapeDtypeStruct((N_GRP, 128, 128), BF16),
        ),
        in_specs=[hbm] * 6 + [pl.BlockSpec(memory_space=pltpu.SMEM)],
        out_specs=(hbm,) * 3,
        scratch_shapes=[
            vmem((4, 8, 8, 512), BF16), vmem((27, C, C), BF16), vmem((C, 128), BF16), vmem((1, 512, 128), BF16),
            smem((4, 26), i32), vmem((4, 26), i32), vmem((8, 128), i32),
            smem((4, PEERS), i32), vmem((4, PEERS), i32), vmem((16, 128), i32), smem((16, 128), i32),
            vmem((1024, 128), F32),
            vmem((LOCAL, 16, 256), BF16),
            vmem((TABLE, 16, 256), BF16),
            vmem((NEAR, 4, 16, 256), BF16),
            vmem((NEAR, 4, 16, 256), BF16),
            vmem((8, 128), i32), vmem((N_SUB, 8, 128), i32),
            vmem((128, 128), BF16),
            vmem((N_SUB, 32, 128), BF16), vmem((N_SUB, 32, 128), BF16),
            vmem((512, 512), BF16),
            vmem((9, 256, 128), BF16), vmem((9, 128, 256), BF16),
            vmem((256, 128), F32), vmem((1280, 128), F32),
            vmem((3, 320, 640), BF16),
            vmem((1024, 128), F32),
            vmem((384, 768), BF16),
            vmem((128, 1024), BF16),
            vmem((15 * 320, 128), F32),
            vmem((TERMS + 1, 8, 512), F32),
            vmem((1024, 128), F32),
            vmem((32, 128), BF16), vmem((N_SUB, 32, 128), BF16),
            vmem((N_GRP, 128, 128), F32), vmem((N_GRP, 128, 128), BF16), vmem((N_GRP, 128, 128), BF16),
            vmem((128, 128), F32),
            vmem((N_SUB, 8, 128), F32), vmem((8, 128), F32), vmem((N_SUB, 8, 128), F32),
            vmem((128, 128), BF16),
            vmem((SLOTS + 1, 8, 512), F32),
            vmem((1, 512, 128), BF16), vmem((4, 8, 8, 512), BF16),
        ]
        + [dma(3), dma(NEAR)]
        + [dma(2)] * 7
        + [dma(9), dma(3)],
        compiler_params=pltpu.CompilerParams(
            collective_id=0, has_side_effects=True, vmem_limit_bytes=VMEM_LIMIT
        ),
        name="block",
    )(features, conv_weight, down_weight, cotangent, src_table, send_list[0].T, child_map)
    return pl.pallas_call(
        finish_kernel,
        out_shape=(
            jax.ShapeDtypeStruct((1, 512, 128), BF16),
            jax.ShapeDtypeStruct((4, 8, 8, 512), BF16),
            jax.ShapeDtypeStruct((27, C, C), F32),
            jax.ShapeDtypeStruct((C, 128), F32),
        ),
        in_specs=[hbm] * 3,
        out_specs=(hbm,) * 4,
        scratch_shapes=[
            vmem((1, 512, 128), BF16), vmem((4, 8, 8, 512), BF16),
            vmem((N_GRP, 128, 128), BF16), vmem((27, C, C), F32), vmem((C, 128), F32), dma(3), dma(7),
        ],
        compiler_params=pltpu.CompilerParams(vmem_limit_bytes=VMEM_LIMIT),
        name="finish",
    )(coarse, grad_input, sums)


def solution(mesh):
    both = ("grp", "sub")
    placed = (
        P(both, None, None, None),
        P(),
        P(),
        P(both, None, None),
        P(both, None),
        P(both, None, None),
        P(both),
    )
    return jax.shard_map(
        per_device,
        mesh=mesh,
        in_specs=placed,
        out_specs=(P(both, None, None), P(both, None, None, None), P(), P()),
        check_vma=False,
    )
```
